32 devices in a mesh: space: 8 (over z, y), tensor: 4 (over x, core).
Axes of the slice: x: 2, y: 2, z: 4, core: 2. Of those that a mesh axis runs over, the one named last changes fastest.
Arguments:
- features: bfloat16 [32, 128, 1024], P('space', None, 'tensor'), may hold values from -6 to 6
- depth_kernel: bfloat16 [2, 7, 7, 1024], P(None, None, None, 'tensor'), may hold values from -5 to 5
- norm_gain: float32 [2, 1024], replicated, may hold values from 0.5 to 1.5
- norm_bias: float32 [2, 1024], replicated, may hold values from -3 to 3
- w_expand: bfloat16 [2, 1024, 4096], P(None, None, 'tensor'), may hold values from -0.1875 to 0.1875
- b_expand: float32 [2, 4096], P(None, 'tensor'), may hold values from -3 to 3
- w_reduce: bfloat16 [2, 4096, 1024], P(None, 'tensor'), may hold values from -0.125 to 0.125
- b_reduce: float32 [2, 1024], P(None, 'tensor'), may hold values from -3 to 3
- layer_scale: float32 [2, 1024], P(None, 'tensor'), may hold values from 0.5 to 1.5
Outputs:
- output: bfloat16 [32, 128, 1024], P('space', None, 'tensor')
The draws below stay inside these ranges and needn't reach their ends.
All inputs are finite; a program needn't handle non-finite values.
Results may differ from the reference program's by a relative error of at most 0.023.
Values may be sent and summed in bfloat16 or wider, within the bound.
A program may use at most 64 MiB of HBM per device.

```python
import jax
import jax.numpy as jnp
from jax import lax

D = 1024
FF = 4096
TAPS = 7
BLOCKS = 2
COLS = 128
ROWS = 32
N_TENSOR = 4


def draw_depth_kernel(key, part):
    key_base, key_jitter = jax.random.split(jax.random.fold_in(key, 7))
    base = jnp.clip(jax.random.normal(key_base, (BLOCKS, TAPS, TAPS, D), jnp.float32), -4.0, 4.0) / 7.0
    jitter = jax.random.uniform(key_jitter, (BLOCKS, 1, 1, D), jnp.float32, 0.8, 1.25)
    ladder = jnp.arange(D, dtype=jnp.float32) / D
    scale = 0.3 * jnp.power(10.0, ladder) * jitter
    return (base * scale).astype(jnp.bfloat16)


def strengthened(entries, own_key, source, target, parts, factor):
    def block_of(dim):
        return (jnp.arange(entries.shape[dim]) // (entries.shape[dim] // parts)).reshape((-1,) + (1,) * (entries.ndim - 1 - dim))

    near = jax.random.permutation(own_key, parts)[block_of(target)]
    second = (block_of(target) + parts // 2) % parts
    return jnp.where((block_of(source) == near) | (block_of(source) == second), factor * entries, entries)


def shard_levels(key, extent, shards, least, largest):
    level, own = 1.0, jax.random.fold_in(key, 6)
    for axis_at, shards_of in shards:
        draws = jnp.exp(jax.random.uniform(jax.random.fold_in(own, axis_at), (shards_of,), jnp.float32, least / len(shards), largest / len(shards)))
        level = level * jnp.repeat(draws, extent[axis_at] // shards_of).reshape([-1 if axis == axis_at else 1 for axis in range(len(extent))])
    return level


def scatter_about(own_key, dims, deviation, reach, cuts=(), kind=jnp.bfloat16):
    factor_of = shard_levels(own_key, dims, cuts, -0.22, 0.18) if cuts else 1.0
    drawn = jax.random.normal(own_key, dims, jnp.float32) * deviation * factor_of
    return jnp.minimum(jnp.maximum(drawn, -reach), reach).astype(kind)


def noise_with(rng, shape, spread, limit, cuts, heavy, held_as=jnp.bfloat16):
    values = spread * jax.random.normal(rng, shape, jnp.float32)
    if cuts:
        values = values * shard_levels(rng, shape, cuts, -0.22, 0.18)
    return jnp.clip(strengthened(values, jax.random.fold_in(rng, 3), *heavy), -limit, limit).astype(held_as)


def setup_inputs(seed: int = 0) -> dict:
    splits = jax.random.split(jax.random.key(seed), 10)
    return {
        "features": scatter_about(splits[0], (ROWS, COLS, D), 1.0, 6.0, ((0, 8), (2, 4))),
        "depth_kernel": draw_depth_kernel(jax.random.fold_in(splits[9], 71), 0),
        "norm_gain": jnp.clip(jax.random.uniform(splits[2], (BLOCKS, D), jnp.float32, 0.5, 1.5), 0.5, 1.5),
        "norm_bias": scatter_about(splits[3], (BLOCKS, D), 0.5, 3.0, (), jnp.float32),
        "w_expand": scatter_about(splits[4], (BLOCKS, D, FF), D ** -0.5, 0.1875, ((2, 4),)),
        "b_expand": scatter_about(splits[5], (BLOCKS, FF), 0.5, 3.0, ((1, 4),), jnp.float32),
        "w_reduce": noise_with(splits[6], (BLOCKS, FF, D), FF ** -0.5, 0.125, ((1, 4),), (1, 2, 4, 2.0)),
        "b_reduce": scatter_about(splits[7], (BLOCKS, D), 0.5, 3.0, ((1, 4),), jnp.float32),
        "layer_scale": jnp.clip(0.5 + 1.0 * jax.random.uniform(splits[8], (BLOCKS, D), jnp.float32) ** shard_levels(splits[8], (BLOCKS, D), ((1, 4),), -0.2, 0.2), 0.5, 1.5),
    }


def depthwise(stream, kernel):
    half = TAPS // 2
    height = stream.shape[0]
    width = stream.shape[1]
    padded = jnp.pad(stream.astype(jnp.float32), ((half, half), (half, half), (0, 0)))
    total = jnp.zeros(stream.shape, jnp.float32)
    for row_tap in range(TAPS):
        for col_tap in range(TAPS):
            total = total + padded[row_tap:row_tap + height, col_tap:col_tap + width] * kernel[row_tap, col_tap].astype(jnp.float32)
    return total

def reference(features, depth_kernel, norm_gain, norm_bias, w_expand, b_expand, w_reduce, b_reduce, layer_scale):
    stream = features
    group = FF // N_TENSOR
    for block_id in range(BLOCKS):
        filtered = depthwise(stream, depth_kernel[block_id])
        mean = lax.optimization_barrier(jnp.mean(filtered, axis=-1, keepdims=True))
        centered = filtered - mean
        var = lax.optimization_barrier(jnp.mean(centered * centered, axis=-1, keepdims=True))
        normed = (centered / jnp.sqrt(var + 1e-06) * norm_gain[block_id] + norm_bias[block_id]).astype(jnp.bfloat16)
        reduce_groups = w_reduce[block_id].astype(jnp.float32).reshape(N_TENSOR, group, D)
        expand = w_expand[block_id]
        bias_one = b_expand[block_id]

        def one_row(row_normed):
            preact = jnp.dot(row_normed, expand, preferred_element_type=jnp.float32) + bias_one
            hidden = jax.nn.gelu(preact, approximate=False).astype(jnp.bfloat16)
            grouped = hidden.astype(jnp.float32).reshape(row_normed.shape[0], N_TENSOR, group)
            partial_value = jnp.einsum('wtf,tfc->wtc', grouped, reduce_groups)
            partial_value = lax.optimization_barrier(partial_value.astype(jnp.bfloat16))
            return lax.optimization_barrier(jnp.sum(partial_value.astype(jnp.float32), axis=1))
        mixed = lax.map(one_row, normed)
        stream = (stream.astype(jnp.float32) + layer_scale[block_id] * (mixed + b_reduce[block_id])).astype(jnp.bfloat16)
    return stream
```

```python
import functools

import jax
import jax.numpy as jnp
from jax import lax
from jax.experimental import pallas as pl
from jax.experimental.pallas import tpu as pltpu
from jax.sharding import PartitionSpec as P

D = 1024
TAPS = 7
BLOCKS = 2


def with_halo(x, sides, width):
    for axis, dim in sides:
        devices, length = (lax.axis_size(axis), x.shape[dim])
        up = [(i, (i + 1) % devices) for i in range(devices - 1)]
        down = [(j, i) for i, j in up]
        last = lax.slice_in_dim(x, length - width, length, axis=dim)
        leading = lax.slice_in_dim(x, 0, width, axis=dim)
        before = lax.ppermute(last, axis, up)
        after = lax.ppermute(leading, axis, down)
        x = jnp.concatenate([before, x, after], axis=dim)
    return x


def one_block(stream, kernel, gain, bias, expand, bias_expand, reduce_w, bias_reduce, scale):
    half = TAPS // 2
    height, width, share = stream.shape
    positions = height * width
    padded = with_halo(stream, (("space", 0),), half)
    padded = jnp.pad(padded.astype(jnp.float32), ((0, 0), (half, half), (0, 0)))
    filtered = jnp.zeros(stream.shape, jnp.float32)
    for row_tap in range(TAPS):
        for col_tap in range(TAPS):
            filtered = filtered + padded[
                row_tap : row_tap + height, col_tap : col_tap + width
            ] * kernel[row_tap, col_tap].astype(jnp.float32)
    filtered = filtered.reshape(positions, share)
    offset = lax.axis_index("tensor") * share
    gain_part = lax.dynamic_slice_in_dim(gain, offset, share, 0)
    bias_part = lax.dynamic_slice_in_dim(bias, offset, share, 0)
    sums, squares = lax.psum(
        (jnp.sum(filtered, axis=-1), jnp.sum(filtered * filtered, axis=-1)), "tensor"
    )
    mean = (sums / D)[:, None]
    var = jnp.maximum(squares[:, None] / D - mean * mean, 0.0)
    normed_part = ((filtered - mean) / jnp.sqrt(var + 1e-06) * gain_part + bias_part).astype(
        jnp.bfloat16
    )
    preact = jnp.dot(
        lax.all_gather(normed_part, "tensor", axis=1, tiled=True),
        expand,
        preferred_element_type=jnp.float32,
    )
    hidden = jax.nn.gelu(preact + bias_expand, approximate=False).astype(jnp.bfloat16)
    partial_value = jnp.dot(hidden, reduce_w, preferred_element_type=jnp.float32)
    mixed = lax.psum_scatter(
        partial_value.astype(jnp.bfloat16), "tensor", scatter_dimension=1, tiled=True
    ).astype(jnp.float32)
    updated = stream.reshape(positions, share).astype(jnp.float32) + scale * (mixed + bias_reduce)
    return updated.astype(jnp.bfloat16).reshape(height, width, share)


def per_device(
    features,
    depth_kernel,
    norm_gain,
    norm_bias,
    w_expand,
    b_expand,
    w_reduce,
    b_reduce,
    layer_scale,
):
    stream = features
    for block_id in range(BLOCKS):
        stream = one_block(
            stream,
            depth_kernel[block_id],
            norm_gain[block_id],
            norm_bias[block_id],
            w_expand[block_id],
            b_expand[block_id],
            w_reduce[block_id],
            b_reduce[block_id],
            layer_scale[block_id],
        )
    return stream


MESH = pl.DeviceIdType.MESH
CORES = 4
EXTRA = 16


def shift_down(x, first):
    return jnp.where(first, 0.0, pltpu.roll(x, 1, 0))


def shift_up(x, last):
    return jnp.where(last, 0.0, pltpu.roll(x, x.shape[0] - 1, 0))


def blocks_kernel(
    n_space, feat, taps, gain, nbias, w1_hbm, b1, w2_hbm, b2, scale, out,
    w1, w2, taps32, xf, filt, mid, halo, gathered, normed, hidden,
    pair_out, pair_in, cross_out, cross_in, own,
    w_sem, halo_send, halo_recv, ag_send, ag_recv, pair_send, pair_recv, cross_send, cross_recv,
):
    rows, width, share = feat.shape
    half = TAPS // 2
    blocks = taps.shape[0]
    band = lax.axis_index("space")
    me = lax.axis_index("tensor")
    core = lax.rem(me, 2)
    mate = me + 1 - 2 * core
    across = lax.rem(me + 2, CORES)
    diagonal = lax.rem(mate + 2, CORES)
    has_up = band > 0
    has_down = band < n_space - 1

    def weight_copies(b):
        return (
            pltpu.make_async_copy(w1_hbm.at[b], w1.at[b], w_sem.at[b, 0]),
            pltpu.make_async_copy(w2_hbm.at[b], w2.at[b], w_sem.at[b, 1]),
        )

    for b in range(blocks):
        for copy in weight_copies(b):
            copy.start()

    barrier = pltpu.get_barrier_semaphore()
    for who in (mate, across):
        pl.semaphore_signal(barrier, inc=1, device_id=(band, who), device_id_type=MESH)

    @pl.when(has_up)
    def _():
        pl.semaphore_signal(barrier, inc=1, device_id=(band - 1, me), device_id_type=MESH)

    @pl.when(has_down)
    def _():
        pl.semaphore_signal(barrier, inc=1, device_id=(band + 1, me), device_id_type=MESH)

    pl.semaphore_wait(barrier, 2 + jnp.minimum(band, 1) + jnp.minimum(n_space - 1 - band, 1))

    def remote(src, dst, send, recv, who):
        return pltpu.make_async_remote_copy(
            src_ref=src, dst_ref=dst, send_sem=send, recv_sem=recv, device_id=who, device_id_type=MESH
        )

    def halo_copy(b, source, side, i):
        row = i if side == 0 else rows - half + i
        target = (band - 1, me) if side == 0 else (band + 1, me)
        return remote(
            source.at[row], halo.at[b, side, i], halo_send.at[b, side, i], halo_recv.at[b, side, i], target
        )

    present = (has_up, has_down)

    def ag_copy(b, r, kind):
        slot, target = ((me, mate), (me, across), (across, mate))[kind]
        ref = gathered.at[b, r, slot]
        return remote(ref, ref, ag_send.at[b, r, kind], ag_recv.at[b, r, kind], (band, target))

    def pair_copy(b, r):
        return remote(
            pair_out.at[b, r], pair_in.at[b, r], pair_send.at[b, r], pair_recv.at[b, r], (band, mate)
        )

    def cross_copy(b, r):
        return remote(
            cross_out.at[b, r], cross_in.at[b, r], cross_send.at[b, r], cross_recv.at[b, r], (band, across)
        )

    column = lax.broadcasted_iota(jnp.int32, (width, 128), 0)
    lane = lax.broadcasted_iota(jnp.int32, (width, 128), 1)
    first, last, diag = column == 0, column == width - 1, column == lane

    def convolve(b, r, pairs):
        def part(h, fresh):
            ch = pl.ds(pl.multiple_of(h * 128, 128), 128)

            def along(j):
                total = None
                for row, tap in pairs:
                    term = xf[row, :, ch] * taps32[b, tap, pl.ds(j, 1), ch]
                    total = term if total is None else total + term
                return total

            right = shift_down(along(0), first)
            for j in range(1, half):
                right = shift_down(right + along(j), first)
            left = shift_up(along(TAPS - 1), last)
            for j in range(TAPS - 2, half, -1):
                left = shift_up(left + along(j), last)
            total = along(half) + right + left
            if not fresh:
                total = total + filt[r, :, ch]
            filt[r, :, ch] = total

        return part

    def conv_own(b):
        def body(step, carry):
            r, h = step // (share // 128), lax.rem(step, share // 128)
            convolve(b, r, [(half + m, half + m - r) for m in range(rows)])(h, True)
            return carry

        lax.fori_loop(0, rows * (share // 128), body, 0)

    def conv_halo(b, r):
        pairs = []
        for m in range(half):
            row = r + m + rows * ((r + m) // half)
            pairs.append((row, row - r))

        def body(h, carry):
            convolve(b, r, pairs)(h, False)
            return carry

        lax.fori_loop(0, share // 128, body, 0)

    def take_halo(b, upper):
        side, base, there = (1, 0, has_up) if upper else (0, half + rows, has_down)

        @pl.when(there)
        def _():
            for i in range(half):
                halo_copy(b, feat, side, i).wait_recv()
            xf[pl.ds(base, half)] = halo[b, side].astype(jnp.float32)

        @pl.when(jnp.logical_not(there))
        def _():
            xf[pl.ds(base, half)] = jnp.zeros((half, width, share), jnp.float32)

    def send_filtered(b, r):
        value = filt[r]
        center = jnp.sum(value, axis=1, keepdims=True) / share
        gathered[b, r, me, pl.ds(0, width), :] = (value - center).astype(jnp.bfloat16)
        line = jnp.sum(jnp.where(diag, center, 0.0), axis=0, keepdims=True)
        high = line.astype(jnp.bfloat16)
        low = (line - high.astype(jnp.float32)).astype(jnp.bfloat16)
        gathered[b, r, me, pl.ds(width, EXTRA), pl.ds(0, width)] = jnp.broadcast_to(high, (EXTRA, width))
        gathered[b, r, me, pl.ds(width, EXTRA), pl.ds(width, width)] = jnp.broadcast_to(low, (EXTRA, width))
        ag_copy(b, r, 1).start()
        ag_copy(b, r, 0).start()

    def normalize(b, r):
        centers = []
        for s in range(CORES):
            tail = gathered[b, r, s, pl.ds(width, EXTRA), :].astype(jnp.float32)
            line = tail[:1, :width] + tail[:1, width:]
            centers.append(jnp.sum(jnp.where(diag, line, 0.0), axis=1, keepdims=True))
        mean = (centers[0] + centers[1] + centers[2] + centers[3]) / CORES
        deltas = [c - mean for c in centers]
        squares = jnp.zeros((width, 1), jnp.float32)
        for s in range(CORES):
            value = gathered[b, r, s, pl.ds(0, width), :].astype(jnp.float32) + deltas[s]
            squares = squares + jnp.sum(value * value, axis=1, keepdims=True)
        inverse = lax.rsqrt(squares / (share * CORES) + 1e-06)
        for s in range(CORES):
            ch = pl.ds(s * share, share)
            value = gathered[b, r, s, pl.ds(0, width), :].astype(jnp.float32) + deltas[s]
            value = value * inverse * gain[pl.ds(b, 1), ch] + nbias[pl.ds(b, 1), ch]
            normed[:, ch] = value.astype(jnp.bfloat16)

    def expand(b):
        for n in range(w1.shape[2] // 256):
            ch = pl.ds(n * 256, 256)
            x = jnp.dot(normed[...], w1[b, :, ch], preferred_element_type=jnp.float32) + b1[pl.ds(b, 1), ch]
            hidden[:, ch] = (0.5 * x * (1.0 + lax.erf(x * 0.7071067811865476))).astype(jnp.bfloat16)

    def reduce_to(b, owner):
        ch = pl.ds(pl.multiple_of(owner * share, share), share)
        return jnp.dot(hidden[...], w2[b, :, ch], preferred_element_type=jnp.float32)

    def pair_sum(b, r):
        pair_copy(b, r).wait_recv()
        total = cross_out[b, r].astype(jnp.float32) + pair_in[b, r, 1].astype(jnp.float32)
        cross_out[b, r] = total.astype(jnp.bfloat16)
        cross_copy(b, r).start()

    def finish(b, r):
        cross_copy(b, r).wait_recv()
        mixed = own[r] + pair_in[b, r, 0].astype(jnp.float32) + cross_in[b, r].astype(jnp.float32)
        before = (feat if b == 0 else mid)[r].astype(jnp.float32)
        new = (before + scale[pl.ds(b, 1), :] * (mixed + b2[pl.ds(b, 1), :])).astype(jnp.bfloat16)
        if b == blocks - 1:
            out[r] = new
            return
        mid[r] = new
        xf[half + r] = new.astype(jnp.float32)

    def send_halo_row(b, source, r):
        if r < half:
            @pl.when(has_up)
            def _():
                halo_copy(b, source, 0, r).start()
        if r >= rows - half:
            @pl.when(has_down)
            def _():
                halo_copy(b, source, 1, r - (rows - half)).start()

    for r in range(rows):
        send_halo_row(0, feat, r)
    taps32[...] = taps[...].astype(jnp.float32)
    for r in range(rows):
        xf[half + r] = feat[r].astype(jnp.float32)

    for b in range(blocks):
        row_of = (lambda k: k) if b == 0 else (lambda k: rows - 1 - k)
        conv_own(b)

        def front(k, carry, b=b, row_of=row_of):
            r = row_of(k)

            @pl.when(k == 0)
            def _():
                take_halo(b, b == 0)

            @pl.when(k == 1)
            def _():
                take_halo(b, b != 0)

            conv_halo(b, r)
            send_filtered(b, r)
            return carry

        lax.fori_loop(0, rows, front, 0)
        for copy in weight_copies(b):
            copy.wait()

        def relay(r, b=b):
            ag_copy(b, r, 1).wait_recv()
            ag_copy(b, r, 2).start()

        relay(row_of(0))

        def middle(k, carry, b=b, row_of=row_of, relay=relay):
            r = row_of(k)
            ag_copy(b, r, 0).wait_recv()
            ag_copy(b, r, 2).wait_recv()
            normalize(b, r)
            expand(b)

            @pl.when(k < rows - 1)
            def _():
                relay(row_of(k + 1))

            @pl.when(k > 0)
            def _():
                pair_sum(b, row_of(k - 1))

            pair_out[b, r, 0] = reduce_to(b, mate).astype(jnp.bfloat16)
            pair_out[b, r, 1] = reduce_to(b, diagonal).astype(jnp.bfloat16)
            pair_copy(b, r).start()
            own[r] = reduce_to(b, me)
            cross_out[b, r] = reduce_to(b, across).astype(jnp.bfloat16)
            return carry

        lax.fori_loop(0, rows, middle, 0)
        pair_sum(b, row_of(rows - 1))
        for k in range(rows):
            finish(b, row_of(k))
            if b < blocks - 1:
                send_halo_row(b + 1, mid, row_of(k))

    for b in range(blocks):
        for side in range(2):
            @pl.when(present[side])
            def _(b=b, side=side):
                for i in range(half):
                    halo_copy(b, feat if b == 0 else mid, side, i).wait_send()

        def drain(r, carry, b=b):
            for kind in range(3):
                ag_copy(b, r, kind).wait_send()
            pair_copy(b, r).wait_send()
            cross_copy(b, r).wait_send()
            return carry

        lax.fori_loop(0, rows, drain, 0)


def fused(n_space, features, depth_kernel, gain, nbias, w1, b1, w2, b2, scale):
    rows, width, share = features.shape
    blocks, depth, units = w1.shape
    half = TAPS // 2
    vmem = pl.BlockSpec(memory_space=pltpu.VMEM)
    hbm = pl.BlockSpec(memory_space=pl.ANY)
    bf, f32 = jnp.bfloat16, jnp.float32
    dma = pltpu.SemaphoreType.DMA
    return pl.pallas_call(
        functools.partial(blocks_kernel, n_space),
        out_shape=jax.ShapeDtypeStruct(features.shape, bf),
        in_specs=[vmem, vmem, vmem, vmem, hbm, vmem, hbm, vmem, vmem],
        out_specs=vmem,
        scratch_shapes=[
            pltpu.VMEM(w1.shape, bf),
            pltpu.VMEM(w2.shape, bf),
            pltpu.VMEM(depth_kernel.shape, f32),
            pltpu.VMEM((rows + 2 * half, width, share), f32),
            pltpu.VMEM((rows, width, share), f32),
            pltpu.VMEM((rows, width, share), bf),
            pltpu.VMEM((blocks, 2, half, width, share), bf),
            pltpu.VMEM((blocks, rows, CORES, width + EXTRA, share), bf),
            pltpu.VMEM((width, depth), bf),
            pltpu.VMEM((width, units), bf),
            pltpu.VMEM((blocks, rows, 2, width, share), bf),
            pltpu.VMEM((blocks, rows, 2, width, share), bf),
            pltpu.VMEM((blocks, rows, width, share), bf),
            pltpu.VMEM((blocks, rows, width, share), bf),
            pltpu.VMEM((rows, width, share), f32),
            dma((blocks, 2)),
            dma((blocks, 2, half)),
            dma((blocks, 2, half)),
            dma((blocks, rows, 3)),
            dma((blocks, rows, 3)),
            dma((blocks, rows)),
            dma((blocks, rows)),
            dma((blocks, rows)),
            dma((blocks, rows)),
        ],
        compiler_params=pltpu.CompilerParams(
            collective_id=0, has_side_effects=True, vmem_limit_bytes=40 * 1024 * 1024
        ),
    )(features, depth_kernel, gain, nbias, w1, b1, w2, b2, scale)


def solution(mesh):
    body = per_device
    if mesh.shape["tensor"] == CORES:
        body = functools.partial(fused, mesh.shape["space"])
    return jax.shard_map(
        body,
        mesh=mesh,
        in_specs=(
            P("space", None, "tensor"),
            P(None, None, None, "tensor"),
            P(),
            P(),
            P(None, None, "tensor"),
            P(None, "tensor"),
            P(None, "tensor", None),
            P(None, "tensor"),
            P(None, "tensor"),
        ),
        out_specs=P("space", None, "tensor"),
        check_vma=False,
    )
```

```python
import functools

import jax
import jax.numpy as jnp
from jax import lax
from jax.experimental import pallas as pl
from jax.experimental.pallas import tpu as pltpu
from jax.sharding import PartitionSpec as P

D = 1024
TAPS = 7
BLOCKS = 2


def with_halo(x, sides, width):
    for axis, dim in sides:
        devices, length = (lax.axis_size(axis), x.shape[dim])
        up = [(i, (i + 1) % devices) for i in range(devices - 1)]
        down = [(j, i) for i, j in up]
        last = lax.slice_in_dim(x, length - width, length, axis=dim)
        leading = lax.slice_in_dim(x, 0, width, axis=dim)
        before = lax.ppermute(last, axis, up)
        after = lax.ppermute(leading, axis, down)
        x = jnp.concatenate([before, x, after], axis=dim)
    return x


def one_block(stream, kernel, gain, bias, expand, bias_expand, reduce_w, bias_reduce, scale):
    half = TAPS // 2
    height, width, share = stream.shape
    positions = height * width
    padded = with_halo(stream, (("space", 0),), half)
    padded = jnp.pad(padded.astype(jnp.float32), ((0, 0), (half, half), (0, 0)))
    filtered = jnp.zeros(stream.shape, jnp.float32)
    for row_tap in range(TAPS):
        for col_tap in range(TAPS):
            filtered = filtered + padded[
                row_tap : row_tap + height, col_tap : col_tap + width
            ] * kernel[row_tap, col_tap].astype(jnp.float32)
    filtered = filtered.reshape(positions, share)
    offset = lax.axis_index("tensor") * share
    gain_part = lax.dynamic_slice_in_dim(gain, offset, share, 0)
    bias_part = lax.dynamic_slice_in_dim(bias, offset, share, 0)
    sums, squares = lax.psum(
        (jnp.sum(filtered, axis=-1), jnp.sum(filtered * filtered, axis=-1)), "tensor"
    )
    mean = (sums / D)[:, None]
    var = jnp.maximum(squares[:, None] / D - mean * mean, 0.0)
    normed_part = ((filtered - mean) / jnp.sqrt(var + 1e-06) * gain_part + bias_part).astype(
        jnp.bfloat16
    )
    preact = jnp.dot(
        lax.all_gather(normed_part, "tensor", axis=1, tiled=True),
        expand,
        preferred_element_type=jnp.float32,
    )
    hidden = jax.nn.gelu(preact + bias_expand, approximate=False).astype(jnp.bfloat16)
    partial_value = jnp.dot(hidden, reduce_w, preferred_element_type=jnp.float32)
    mixed = lax.psum_scatter(
        partial_value.astype(jnp.bfloat16), "tensor", scatter_dimension=1, tiled=True
    ).astype(jnp.float32)
    updated = stream.reshape(positions, share).astype(jnp.float32) + scale * (mixed + bias_reduce)
    return updated.astype(jnp.bfloat16).reshape(height, width, share)


def per_device(
    features,
    depth_kernel,
    norm_gain,
    norm_bias,
    w_expand,
    b_expand,
    w_reduce,
    b_reduce,
    layer_scale,
):
    stream = features
    for block_id in range(BLOCKS):
        stream = one_block(
            stream,
            depth_kernel[block_id],
            norm_gain[block_id],
            norm_bias[block_id],
            w_expand[block_id],
            b_expand[block_id],
            w_reduce[block_id],
            b_reduce[block_id],
            layer_scale[block_id],
        )
    return stream


MESH = pl.DeviceIdType.MESH
CORES = 4
EXTRA = 16


def shift_down(x, first):
    return jnp.where(first, 0.0, pltpu.roll(x, 1, 0))


def shift_up(x, last):
    return jnp.where(last, 0.0, pltpu.roll(x, x.shape[0] - 1, 0))


def blocks_kernel(
    n_space, feat_in, taps_in, gain_in, nbias_in, w1_in, b1_in, w2_in, b2_in, scale_in, out,
    feat, taps, gain, nbias, w1, b1, w2, b2, scale, taps32, xf, filt, mid, halo, gathered, normed, hidden,
    pair_out, pair_in, cross_out, cross_in, own,
    w_sem, in_sem, halo_send, halo_recv, ag_send, ag_recv, pair_send, pair_recv, cross_send, cross_recv,
):
    rows, width, share = feat.shape
    half = TAPS // 2
    blocks = w1.shape[0]
    band = lax.axis_index("space")
    me = lax.axis_index("tensor")
    core = lax.rem(me, 2)
    mate = me + 1 - 2 * core
    across = lax.rem(me + 2, CORES)
    diagonal = lax.rem(mate + 2, CORES)
    has_up = band > 0
    has_down = band < n_space - 1

    def weight_copies(b):
        return (
            pltpu.make_async_copy(w1_in.at[b], w1.at[b], w_sem.at[b, 0]),
            pltpu.make_async_copy(w2_in.at[b], w2.at[b], w_sem.at[b, 1]),
        )

    pairs_in = (
        (feat_in, feat), (taps_in, taps), (gain_in, gain), (nbias_in, nbias),
        (b1_in, b1), (b2_in, b2), (scale_in, scale),
    )
    small_copies = [
        pltpu.make_async_copy(src, dst, in_sem.at[i]) for i, (src, dst) in enumerate(pairs_in)
    ]
    for copy in small_copies:
        copy.start()
    for b in range(blocks):
        for copy in weight_copies(b):
            copy.start()

    barrier = pltpu.get_barrier_semaphore()
    for who in (mate, across):
        pl.semaphore_signal(barrier, inc=1, device_id=(band, who), device_id_type=MESH)

    @pl.when(has_up)
    def _():
        pl.semaphore_signal(barrier, inc=1, device_id=(band - 1, me), device_id_type=MESH)

    @pl.when(has_down)
    def _():
        pl.semaphore_signal(barrier, inc=1, device_id=(band + 1, me), device_id_type=MESH)

    pl.semaphore_wait(barrier, 2 + jnp.minimum(band, 1) + jnp.minimum(n_space - 1 - band, 1))

    def remote(src, dst, send, recv, who):
        return pltpu.make_async_remote_copy(
            src_ref=src, dst_ref=dst, send_sem=send, recv_sem=recv, device_id=who, device_id_type=MESH
        )

    def halo_copy(b, source, side, i):
        row = i if side == 0 else rows - half + i
        target = (band - 1, me) if side == 0 else (band + 1, me)
        return remote(
            source.at[row], halo.at[b, side, i], halo_send.at[b, side, i], halo_recv.at[b, side, i], target
        )

    present = (has_up, has_down)

    def ag_copy(b, r, kind):
        slot, target = ((me, mate), (me, across), (across, mate))[kind]
        ref = gathered.at[b, r, slot]
        return remote(ref, ref, ag_send.at[b, r, kind], ag_recv.at[b, r, kind], (band, target))

    def pair_copy(b, r):
        return remote(
            pair_out.at[b, r], pair_in.at[b, r], pair_send.at[b, r], pair_recv.at[b, r], (band, mate)
        )

    def cross_copy(b, r):
        return remote(
            cross_out.at[b, r], cross_in.at[b, r], cross_send.at[b, r], cross_recv.at[b, r], (band, across)
        )

    column = lax.broadcasted_iota(jnp.int32, (width, 128), 0)
    lane = lax.broadcasted_iota(jnp.int32, (width, 128), 1)
    first, last, diag = column == 0, column == width - 1, column == lane

    def convolve(b, r, pairs):
        def part(h, fresh):
            ch = pl.ds(pl.multiple_of(h * 128, 128), 128)

            def along(j):
                total = None
                for row, tap in pairs:
                    term = xf[row, :, ch] * taps32[b, tap, pl.ds(j, 1), ch]
                    total = term if total is None else total + term
                return total

            right = shift_down(along(0), first)
            for j in range(1, half):
                right = shift_down(right + along(j), first)
            left = shift_up(along(TAPS - 1), last)
            for j in range(TAPS - 2, half, -1):
                left = shift_up(left + along(j), last)
            total = along(half) + right + left
            if not fresh:
                total = total + filt[r, :, ch]
            filt[r, :, ch] = total

        return part

    def conv_own(b):
        def body(step, carry):
            r, h = step // (share // 128), lax.rem(step, share // 128)
            convolve(b, r, [(half + m, half + m - r) for m in range(rows)])(h, True)
            return carry

        lax.fori_loop(0, rows * (share // 128), body, 0)

    def conv_halo(b, r):
        pairs = []
        for m in range(half):
            row = r + m + rows * ((r + m) // half)
            pairs.append((row, row - r))

        def body(h, carry):
            convolve(b, r, pairs)(h, False)
            return carry

        lax.fori_loop(0, share // 128, body, 0)

    def take_halo(b, upper):
        side, base, there = (1, 0, has_up) if upper else (0, half + rows, has_down)

        @pl.when(there)
        def _():
            for i in range(half):
                halo_copy(b, mid, side, i).wait_recv()
            xf[pl.ds(base, half)] = halo[b, side].astype(jnp.float32)

        @pl.when(jnp.logical_not(there))
        def _():
            xf[pl.ds(base, half)] = jnp.zeros((half, width, share), jnp.float32)

    def send_filtered(b, r):
        value = filt[r]
        center = jnp.sum(value, axis=1, keepdims=True) / share
        gathered[b, r, me, pl.ds(0, width), :] = (value - center).astype(jnp.bfloat16)
        line = jnp.sum(jnp.where(diag, center, 0.0), axis=0, keepdims=True)
        high = line.astype(jnp.bfloat16)
        low = (line - high.astype(jnp.float32)).astype(jnp.bfloat16)
        gathered[b, r, me, pl.ds(width, EXTRA), pl.ds(0, width)] = jnp.broadcast_to(high, (EXTRA, width))
        gathered[b, r, me, pl.ds(width, EXTRA), pl.ds(width, width)] = jnp.broadcast_to(low, (EXTRA, width))
        ag_copy(b, r, 1).start()
        ag_copy(b, r, 0).start()

    def normalize(b, r):
        centers = []
        for s in range(CORES):
            tail = gathered[b, r, s, pl.ds(width, EXTRA), :].astype(jnp.float32)
            line = tail[:1, :width] + tail[:1, width:]
            centers.append(jnp.sum(jnp.where(diag, line, 0.0), axis=1, keepdims=True))
        mean = (centers[0] + centers[1] + centers[2] + centers[3]) / CORES
        deltas = [c - mean for c in centers]
        squares = jnp.zeros((width, 1), jnp.float32)
        for s in range(CORES):
            value = gathered[b, r, s, pl.ds(0, width), :].astype(jnp.float32) + deltas[s]
            squares = squares + jnp.sum(value * value, axis=1, keepdims=True)
        inverse = lax.rsqrt(squares / (share * CORES) + 1e-06)
        for s in range(CORES):
            ch = pl.ds(s * share, share)
            value = gathered[b, r, s, pl.ds(0, width), :].astype(jnp.float32) + deltas[s]
            value = value * inverse * gain[pl.ds(b, 1), ch] + nbias[pl.ds(b, 1), ch]
            normed[:, ch] = value.astype(jnp.bfloat16)

    def expand(b):
        for n in range(w1.shape[2] // 256):
            ch = pl.ds(n * 256, 256)
            x = jnp.dot(normed[...], w1[b, :, ch], preferred_element_type=jnp.float32) + b1[pl.ds(b, 1), ch]
            hidden[:, ch] = (0.5 * x * (1.0 + lax.erf(x * 0.7071067811865476))).astype(jnp.bfloat16)

    def reduce_to(b, owner):
        ch = pl.ds(pl.multiple_of(owner * share, share), share)
        return jnp.dot(hidden[...], w2[b, :, ch], preferred_element_type=jnp.float32)

    def pair_sum(b, r):
        pair_copy(b, r).wait_recv()
        total = cross_out[b, r].astype(jnp.float32) + pair_in[b, r, 1].astype(jnp.float32)
        cross_out[b, r] = total.astype(jnp.bfloat16)
        cross_copy(b, r).start()

    def finish(b, r):
        cross_copy(b, r).wait_recv()
        mixed = own[r] + pair_in[b, r, 0].astype(jnp.float32) + cross_in[b, r].astype(jnp.float32)
        before = (feat if b == 0 else mid)[r].astype(jnp.float32)
        new = (before + scale[pl.ds(b, 1), :] * (mixed + b2[pl.ds(b, 1), :])).astype(jnp.bfloat16)
        if b == blocks - 1:
            out[r] = new
            return
        mid[r] = new
        xf[half + r] = new.astype(jnp.float32)

    def send_halo_row(b, source, r):
        if r < half:
            @pl.when(has_up)
            def _():
                halo_copy(b, source, 0, r).start()
        if r >= rows - half:
            @pl.when(has_down)
            def _():
                halo_copy(b, source, 1, r - (rows - half)).start()

    for r in range(rows):
        send_halo_row(0, feat_in, r)
    for copy in small_copies:
        copy.wait()
    for b in range(blocks):
        taps32[b] = taps[:, :, b, :].astype(jnp.float32)
    for r in range(rows):
        xf[half + r] = feat[r].astype(jnp.float32)

    for b in range(blocks):
        row_of = (lambda k: k) if b == 0 else (lambda k: rows - 1 - k)
        conv_own(b)

        def front(k, carry, b=b, row_of=row_of):
            r = row_of(k)

            @pl.when(k == 0)
            def _():
                take_halo(b, b == 0)

            @pl.when(k == 1)
            def _():
                take_halo(b, b != 0)

            conv_halo(b, r)
            send_filtered(b, r)
            return carry

        lax.fori_loop(0, rows, front, 0)
        for copy in weight_copies(b):
            copy.wait()

        def relay(r, b=b):
            ag_copy(b, r, 1).wait_recv()
            ag_copy(b, r, 2).start()

        relay(row_of(0))

        def middle(k, carry, b=b, row_of=row_of, relay=relay):
            r = row_of(k)
            ag_copy(b, r, 0).wait_recv()
            ag_copy(b, r, 2).wait_recv()
            normalize(b, r)
            expand(b)

            @pl.when(k < rows - 1)
            def _():
                relay(row_of(k + 1))

            @pl.when(k > 0)
            def _():
                pair_sum(b, row_of(k - 1))

            pair_out[b, r, 0] = reduce_to(b, mate).astype(jnp.bfloat16)
            pair_out[b, r, 1] = reduce_to(b, diagonal).astype(jnp.bfloat16)
            pair_copy(b, r).start()
            own[r] = reduce_to(b, me)
            cross_out[b, r] = reduce_to(b, across).astype(jnp.bfloat16)
            return carry

        lax.fori_loop(0, rows, middle, 0)
        pair_sum(b, row_of(rows - 1))
        for k in range(rows):
            finish(b, row_of(k))
            if b < blocks - 1:
                send_halo_row(b + 1, mid, row_of(k))

    for b in range(blocks):
        for side in range(2):
            @pl.when(present[side])
            def _(b=b, side=side):
                for i in range(half):
                    halo_copy(b, feat_in if b == 0 else mid, side, i).wait_send()

        def drain(r, carry, b=b):
            for kind in range(3):
                ag_copy(b, r, kind).wait_send()
            pair_copy(b, r).wait_send()
            cross_copy(b, r).wait_send()
            return carry

        lax.fori_loop(0, rows, drain, 0)


def fused(n_space, features, depth_kernel, gain, nbias, w1, b1, w2, b2, scale):
    rows, width, share = features.shape
    blocks, depth, units = w1.shape
    half = TAPS // 2
    depth_kernel = jnp.transpose(depth_kernel, (1, 2, 0, 3))
    operands = (features, depth_kernel, gain, nbias, w1, b1, w2, b2, scale)
    vmem = pl.BlockSpec(memory_space=pltpu.VMEM)
    hbm = pl.BlockSpec(memory_space=pl.ANY)
    bf, f32 = jnp.bfloat16, jnp.float32
    dma = pltpu.SemaphoreType.DMA
    return pl.pallas_call(
        functools.partial(blocks_kernel, n_space),
        out_shape=jax.ShapeDtypeStruct(features.shape, bf),
        in_specs=[hbm] * len(operands),
        out_specs=vmem,
        scratch_shapes=[
            *[pltpu.VMEM(a.shape, a.dtype) for a in operands],
            pltpu.VMEM((blocks, TAPS, TAPS, share), f32),
            pltpu.VMEM((rows + 2 * half, width, share), f32),
            pltpu.VMEM((rows, width, share), f32),
            pltpu.VMEM((rows, width, share), bf),
            pltpu.VMEM((blocks, 2, half, width, share), bf),
            pltpu.VMEM((blocks, rows, CORES, width + EXTRA, share), bf),
            pltpu.VMEM((width, depth), bf),
            pltpu.VMEM((width, units), bf),
            pltpu.VMEM((blocks, rows, 2, width, share), bf),
            pltpu.VMEM((blocks, rows, 2, width, share), bf),
            pltpu.VMEM((blocks, rows, width, share), bf),
            pltpu.VMEM((blocks, rows, width, share), bf),
            pltpu.VMEM((rows, width, share), f32),
            dma((blocks, 2)),
            dma((7,)),
            dma((blocks, 2, half)),
            dma((blocks, 2, half)),
            dma((blocks, rows, 3)),
            dma((blocks, rows, 3)),
            dma((blocks, rows)),
            dma((blocks, rows)),
            dma((blocks, rows)),
            dma((blocks, rows)),
        ],
        compiler_params=pltpu.CompilerParams(
            collective_id=0, has_side_effects=True, vmem_limit_bytes=64 * 1024 * 1024
        ),
    )(*operands)


def solution(mesh):
    body = per_device
    if mesh.shape["tensor"] == CORES:
        body = functools.partial(fused, mesh.shape["space"])
    return jax.shard_map(
        body,
        mesh=mesh,
        in_specs=(
            P("space", None, "tensor"),
            P(None, None, None, "tensor"),
            P(),
            P(),
            P(None, None, "tensor"),
            P(None, "tensor"),
            P(None, "tensor", None),
            P(None, "tensor"),
            P(None, "tensor"),
        ),
        out_specs=P("space", None, "tensor"),
        check_vma=False,
    )
```

```python
import functools

import jax
import jax.numpy as jnp
from jax import lax
from jax.experimental import pallas as pl
from jax.experimental.pallas import tpu as pltpu
from jax.sharding import PartitionSpec as P

D = 1024
TAPS = 7
BLOCKS = 2


def with_halo(x, sides, width):
    for axis, dim in sides:
        devices, length = (lax.axis_size(axis), x.shape[dim])
        up = [(i, (i + 1) % devices) for i in range(devices - 1)]
        down = [(j, i) for i, j in up]
        last = lax.slice_in_dim(x, length - width, length, axis=dim)
        leading = lax.slice_in_dim(x, 0, width, axis=dim)
        before = lax.ppermute(last, axis, up)
        after = lax.ppermute(leading, axis, down)
        x = jnp.concatenate([before, x, after], axis=dim)
    return x


def one_block(stream, kernel, gain, bias, expand, bias_expand, reduce_w, bias_reduce, scale):
    half = TAPS // 2
    height, width, share = stream.shape
    positions = height * width
    padded = with_halo(stream, (("space", 0),), half)
    padded = jnp.pad(padded.astype(jnp.float32), ((0, 0), (half, half), (0, 0)))
    filtered = jnp.zeros(stream.shape, jnp.float32)
    for row_tap in range(TAPS):
        for col_tap in range(TAPS):
            filtered = filtered + padded[
                row_tap : row_tap + height, col_tap : col_tap + width
            ] * kernel[row_tap, col_tap].astype(jnp.float32)
    filtered = filtered.reshape(positions, share)
    offset = lax.axis_index("tensor") * share
    gain_part = lax.dynamic_slice_in_dim(gain, offset, share, 0)
    bias_part = lax.dynamic_slice_in_dim(bias, offset, share, 0)
    sums, squares = lax.psum(
        (jnp.sum(filtered, axis=-1), jnp.sum(filtered * filtered, axis=-1)), "tensor"
    )
    mean = (sums / D)[:, None]
    var = jnp.maximum(squares[:, None] / D - mean * mean, 0.0)
    normed_part = ((filtered - mean) / jnp.sqrt(var + 1e-06) * gain_part + bias_part).astype(
        jnp.bfloat16
    )
    preact = jnp.dot(
        lax.all_gather(normed_part, "tensor", axis=1, tiled=True),
        expand,
        preferred_element_type=jnp.float32,
    )
    hidden = jax.nn.gelu(preact + bias_expand, approximate=False).astype(jnp.bfloat16)
    partial_value = jnp.dot(hidden, reduce_w, preferred_element_type=jnp.float32)
    mixed = lax.psum_scatter(
        partial_value.astype(jnp.bfloat16), "tensor", scatter_dimension=1, tiled=True
    ).astype(jnp.float32)
    updated = stream.reshape(positions, share).astype(jnp.float32) + scale * (mixed + bias_reduce)
    return updated.astype(jnp.bfloat16).reshape(height, width, share)


def per_device(
    features,
    depth_kernel,
    norm_gain,
    norm_bias,
    w_expand,
    b_expand,
    w_reduce,
    b_reduce,
    layer_scale,
):
    stream = features
    for block_id in range(BLOCKS):
        stream = one_block(
            stream,
            depth_kernel[block_id],
            norm_gain[block_id],
            norm_bias[block_id],
            w_expand[block_id],
            b_expand[block_id],
            w_reduce[block_id],
            b_reduce[block_id],
            layer_scale[block_id],
        )
    return stream


MESH = pl.DeviceIdType.MESH
CORES = 4


def shift_down(x, first):
    return jnp.where(first, 0.0, pltpu.roll(x, 1, 0))


def shift_up(x, last):
    return jnp.where(last, 0.0, pltpu.roll(x, x.shape[0] - 1, 0))


def blocks_kernel(
    n_space, feat_in, taps_in, gain_in, nbias_in, w1_in, b1_in, w2_in, b2_in, scale_in, out,
    feat, taps, gain, nbias, w1, b1, w2, b2, scale, taps32, xf, filt, mid, halo, gathered, centers, normed, hidden,
    pair_out, pair_in, cross_out, cross_in, own,
    w_sem, in_sem, halo_send, halo_recv, ag_send, ag_recv, pair_send, pair_recv, cross_send, cross_recv,
):
    rows, width, share = feat.shape
    half = TAPS // 2
    blocks = w1.shape[0]
    band = lax.axis_index("space")
    me = lax.axis_index("tensor")
    core = lax.rem(me, 2)
    mate = me + 1 - 2 * core
    across = lax.rem(me + 2, CORES)
    diagonal = lax.rem(mate + 2, CORES)
    has_up = band > 0
    has_down = band < n_space - 1

    def weight_copies(b):
        return (
            pltpu.make_async_copy(w1_in.at[b], w1.at[b], w_sem.at[b, 0]),
            pltpu.make_async_copy(w2_in.at[b], w2.at[b], w_sem.at[b, 1]),
        )

    pairs_in = (
        (feat_in, feat), (taps_in, taps), (gain_in, gain), (nbias_in, nbias),
        (b1_in, b1), (b2_in, b2), (scale_in, scale),
    )
    small_copies = [
        pltpu.make_async_copy(src, dst, in_sem.at[i]) for i, (src, dst) in enumerate(pairs_in)
    ]
    for copy in small_copies:
        copy.start()
    for b in range(blocks):
        for copy in weight_copies(b):
            copy.start()

    barrier = pltpu.get_barrier_semaphore()
    for who in (mate, across):
        pl.semaphore_signal(barrier, inc=1, device_id=(band, who), device_id_type=MESH)

    @pl.when(has_up)
    def _():
        pl.semaphore_signal(barrier, inc=1, device_id=(band - 1, me), device_id_type=MESH)

    @pl.when(has_down)
    def _():
        pl.semaphore_signal(barrier, inc=1, device_id=(band + 1, me), device_id_type=MESH)

    pl.semaphore_wait(barrier, 2 + jnp.minimum(band, 1) + jnp.minimum(n_space - 1 - band, 1))

    def remote(src, dst, send, recv, who):
        return pltpu.make_async_remote_copy(
            src_ref=src, dst_ref=dst, send_sem=send, recv_sem=recv, device_id=who, device_id_type=MESH
        )

    def halo_copy(b, source, side, i):
        row = i if side == 0 else rows - half + i
        target = (band - 1, me) if side == 0 else (band + 1, me)
        return remote(
            source.at[row], halo.at[b, side, i], halo_send.at[b, side, i], halo_recv.at[b, side, i], target
        )

    present = (has_up, has_down)

    def ag_copy(b, r, kind):
        slot, target = ((me, mate), (me, across), (across, mate))[kind % 3]
        ref = (gathered if kind < 3 else centers).at[b, r, slot]
        return remote(ref, ref, ag_send.at[b, r, kind], ag_recv.at[b, r, kind], (band, target))

    def pair_copy(b, r):
        return remote(
            pair_out.at[b, r], pair_in.at[b, r], pair_send.at[b, r], pair_recv.at[b, r], (band, mate)
        )

    def cross_copy(b, r):
        return remote(
            cross_out.at[b, r], cross_in.at[b, r], cross_send.at[b, r], cross_recv.at[b, r], (band, across)
        )

    column = lax.broadcasted_iota(jnp.int32, (width, 128), 0)
    lane = lax.broadcasted_iota(jnp.int32, (width, 128), 1)
    first, last, diag = column == 0, column == width - 1, column == lane

    def convolve(b, r, pairs):
        def part(h, fresh):
            ch = pl.ds(pl.multiple_of(h * 128, 128), 128)

            def along(j):
                total = None
                for row, tap in pairs:
                    term = xf[row, :, ch] * taps32[b, tap, pl.ds(j, 1), ch]
                    total = term if total is None else total + term
                return total

            right = shift_down(along(0), first)
            for j in range(1, half):
                right = shift_down(right + along(j), first)
            left = shift_up(along(TAPS - 1), last)
            for j in range(TAPS - 2, half, -1):
                left = shift_up(left + along(j), last)
            total = along(half) + right + left
            if not fresh:
                total = total + filt[r, :, ch]
            filt[r, :, ch] = total

        return part

    def conv_own(b):
        def body(step, carry):
            r, h = step // (share // 128), lax.rem(step, share // 128)
            convolve(b, r, [(half + m, half + m - r) for m in range(rows)])(h, True)
            return carry

        lax.fori_loop(0, rows * (share // 128), body, 0)

    def conv_halo(b, r):
        pairs = []
        for m in range(half):
            row = r + m + rows * ((r + m) // half)
            pairs.append((row, row - r))

        def body(h, carry):
            convolve(b, r, pairs)(h, False)
            return carry

        lax.fori_loop(0, share // 128, body, 0)

    def take_halo(b, upper, i):
        side, base, there = (1, 0, has_up) if upper else (0, half + rows, has_down)

        @pl.when(there)
        def _():
            halo_copy(b, mid, side, i).wait_recv()
            xf[base + i] = halo[b, side, i].astype(jnp.float32)

        @pl.when(jnp.logical_not(there))
        def _():
            xf[base + i] = jnp.zeros((width, share), jnp.float32)

    def send_filtered(b, r):
        value = filt[r]
        center = jnp.sum(value, axis=1, keepdims=True) / share
        gathered[b, r, me] = (value - center).astype(jnp.bfloat16)
        centers[b, r, me] = jnp.sum(jnp.where(diag, center, 0.0), axis=0, keepdims=True)
        for kind in (4, 1, 3, 0):
            ag_copy(b, r, kind).start()

    def normalize(b, r):
        own_means = [
            jnp.sum(jnp.where(diag, centers[b, r, s], 0.0), axis=1, keepdims=True) for s in range(CORES)
        ]
        mean = (own_means[0] + own_means[1] + own_means[2] + own_means[3]) / CORES
        deltas = [c - mean for c in own_means]
        squares = jnp.zeros((width, 1), jnp.float32)
        for s in range(CORES):
            value = gathered[b, r, s].astype(jnp.float32) + deltas[s]
            squares = squares + jnp.sum(value * value, axis=1, keepdims=True)
        inverse = lax.rsqrt(squares / (share * CORES) + 1e-06)
        for s in range(CORES):
            ch = pl.ds(s * share, share)
            value = gathered[b, r, s].astype(jnp.float32) + deltas[s]
            value = value * inverse * gain[pl.ds(b, 1), ch] + nbias[pl.ds(b, 1), ch]
            normed[:, ch] = value.astype(jnp.bfloat16)

    def expand(b):
        for n in range(w1.shape[2] // 256):
            ch = pl.ds(n * 256, 256)
            x = jnp.dot(normed[...], w1[b, :, ch], preferred_element_type=jnp.float32) + b1[pl.ds(b, 1), ch]
            hidden[:, ch] = (0.5 * x * (1.0 + lax.erf(x * 0.7071067811865476))).astype(jnp.bfloat16)

    def reduce_to(b, owner):
        ch = pl.ds(pl.multiple_of(owner * share, share), share)
        return jnp.dot(hidden[...], w2[b, :, ch], preferred_element_type=jnp.float32)

    def pair_sum(b, r):
        pair_copy(b, r).wait_recv()
        total = cross_out[b, r].astype(jnp.float32) + pair_in[b, r, 1].astype(jnp.float32)
        cross_out[b, r] = total.astype(jnp.bfloat16)
        cross_copy(b, r).start()

    def finish(b, r):
        cross_copy(b, r).wait_recv()
        mixed = own[r] + pair_in[b, r, 0].astype(jnp.float32) + cross_in[b, r].astype(jnp.float32)
        before = (feat if b == 0 else mid)[r].astype(jnp.float32)
        new = (before + scale[pl.ds(b, 1), :] * (mixed + b2[pl.ds(b, 1), :])).astype(jnp.bfloat16)
        if b == blocks - 1:
            out[r] = new
            return
        mid[r] = new
        xf[half + r] = new.astype(jnp.float32)

    def send_halo(b, source, side, i):
        @pl.when(present[side])
        def _():
            halo_copy(b, source, side, i).start()

    for i in range(half):
        send_halo(0, feat_in, 1, i)
    for copy in small_copies:
        copy.wait()
    for b in range(blocks):
        taps32[b] = taps[:, :, b, :].astype(jnp.float32)
    for r in range(rows):
        xf[half + r] = feat[r].astype(jnp.float32)

    for b in range(blocks):
        downward = b % 2 == 0
        row_of = (lambda k: k) if downward else (lambda k: rows - 1 - k)
        conv_own(b)
        if b == 0:
            @pl.when(has_down)
            def _():
                for i in range(half):
                    halo_copy(0, feat_in, 1, i).wait_send()

            for i in range(half):
                send_halo(0, feat_in, 0, i)
        else:
            send_halo(b, mid, 1 if not downward else 0, half - 2 if not downward else 1)

        for i in range(half):
            take_halo(b, downward, i)

        def front(k, carry, b=b, row_of=row_of, downward=downward):
            r = row_of(k)

            @pl.when(k > 0)
            def _():
                take_halo(b, not downward, k - 1 if downward else rows - 1 - k)

            conv_halo(b, r)
            send_filtered(b, r)
            return carry

        if b > 0:
            front(0, 0)
            send_halo(b, mid, 1 if not downward else 0, 0 if not downward else half - 1)
            lax.fori_loop(1, rows, front, 0)
        else:
            lax.fori_loop(0, rows, front, 0)
        for copy in weight_copies(b):
            copy.wait()

        def relay(r, b=b):
            for kind in (4, 1):
                ag_copy(b, r, kind).wait_recv()
                ag_copy(b, r, kind + 1).start()

        relay(row_of(0))

        def middle(k, carry, b=b, row_of=row_of, relay=relay):
            r = row_of(k)
            for kind in (0, 3, 2, 5):
                ag_copy(b, r, kind).wait_recv()
            normalize(b, r)
            expand(b)

            @pl.when(k < rows - 1)
            def _():
                relay(row_of(k + 1))

            @pl.when(k > 0)
            def _():
                pair_sum(b, row_of(k - 1))

            pair_out[b, r, 0] = reduce_to(b, mate).astype(jnp.bfloat16)
            pair_out[b, r, 1] = reduce_to(b, diagonal).astype(jnp.bfloat16)
            pair_copy(b, r).start()
            own[r] = reduce_to(b, me)
            cross_out[b, r] = reduce_to(b, across).astype(jnp.bfloat16)
            return carry

        lax.fori_loop(0, rows, middle, 0)
        pair_sum(b, row_of(rows - 1))
        for k in range(rows):
            r = row_of(k)
            finish(b, r)
            if b == blocks - 1:
                continue
            if downward and r < half:
                send_halo(b + 1, mid, 0, r)
            if not downward and r >= rows - half:
                send_halo(b + 1, mid, 1, r - (rows - half))
            if k == rows - 1:
                send_halo(b + 1, mid, 1 if downward else 0, half - 1 if downward else 0)

    for b in range(blocks):
        for side in range(2):
            if b == 0 and side == 1:
                continue

            @pl.when(present[side])
            def _(b=b, side=side):
                for i in range(half):
                    halo_copy(b, feat_in if b == 0 else mid, side, i).wait_send()

        def drain(r, carry, b=b):
            for kind in range(6):
                ag_copy(b, r, kind).wait_send()
            pair_copy(b, r).wait_send()
            cross_copy(b, r).wait_send()
            return carry

        lax.fori_loop(0, rows, drain, 0)


def fused(n_space, features, depth_kernel, gain, nbias, w1, b1, w2, b2, scale):
    rows, width, share = features.shape
    blocks, depth, units = w1.shape
    half = TAPS // 2
    depth_kernel = jnp.transpose(depth_kernel, (1, 2, 0, 3))
    operands = (features, depth_kernel, gain, nbias, w1, b1, w2, b2, scale)
    vmem = pl.BlockSpec(memory_space=pltpu.VMEM)
    hbm = pl.BlockSpec(memory_space=pl.ANY)
    bf, f32 = jnp.bfloat16, jnp.float32
    dma = pltpu.SemaphoreType.DMA
    return pl.pallas_call(
        functools.partial(blocks_kernel, n_space),
        out_shape=jax.ShapeDtypeStruct(features.shape, bf),
        in_specs=[hbm] * len(operands),
        out_specs=vmem,
        scratch_shapes=[
            *[pltpu.VMEM(a.shape, a.dtype) for a in operands],
            pltpu.VMEM((blocks, TAPS, TAPS, share), f32),
            pltpu.VMEM((rows + 2 * half, width, share), f32),
            pltpu.VMEM((rows, width, share), f32),
            pltpu.VMEM((rows, width, share), bf),
            pltpu.VMEM((blocks, 2, half, width, share), bf),
            pltpu.VMEM((blocks, rows, CORES, width, share), bf),
            pltpu.VMEM((blocks, rows, CORES, 1, width), f32),
            pltpu.VMEM((width, depth), bf),
            pltpu.VMEM((width, units), bf),
            pltpu.VMEM((blocks, rows, 2, width, share), bf),
            pltpu.VMEM((blocks, rows, 2, width, share), bf),
            pltpu.VMEM((blocks, rows, width, share), bf),
            pltpu.VMEM((blocks, rows, width, share), bf),
            pltpu.VMEM((rows, width, share), f32),
            dma((blocks, 2)),
            dma((7,)),
            dma((blocks, 2, half)),
            dma((blocks, 2, half)),
            dma((blocks, rows, 6)),
            dma((blocks, rows, 6)),
            dma((blocks, rows)),
            dma((blocks, rows)),
            dma((blocks, rows)),
            dma((blocks, rows)),
        ],
        compiler_params=pltpu.CompilerParams(
            collective_id=0, has_side_effects=True, vmem_limit_bytes=64 * 1024 * 1024
        ),
    )(*operands)


def solution(mesh):
    body = per_device
    if mesh.shape["tensor"] == CORES:
        body = functools.partial(fused, mesh.shape["space"])
    return jax.shard_map(
        body,
        mesh=mesh,
        in_specs=(
            P("space", None, "tensor"),
            P(None, None, None, "tensor"),
            P(),
            P(),
            P(None, None, "tensor"),
            P(None, "tensor"),
            P(None, "tensor", None),
            P(None, "tensor"),
            P(None, "tensor"),
        ),
        out_specs=P("space", None, "tensor"),
        check_vma=False,
    )
```

```python
import functools

import jax
import jax.numpy as jnp
from jax import lax
from jax.experimental import pallas as pl
from jax.experimental.pallas import tpu as pltpu
from jax.sharding import PartitionSpec as P

D = 1024
TAPS = 7
BLOCKS = 2


def with_halo(x, sides, width):
    for axis, dim in sides:
        devices, length = (lax.axis_size(axis), x.shape[dim])
        up = [(i, (i + 1) % devices) for i in range(devices - 1)]
        down = [(j, i) for i, j in up]
        last = lax.slice_in_dim(x, length - width, length, axis=dim)
        leading = lax.slice_in_dim(x, 0, width, axis=dim)
        before = lax.ppermute(last, axis, up)
        after = lax.ppermute(leading, axis, down)
        x = jnp.concatenate([before, x, after], axis=dim)
    return x


def one_block(stream, kernel, gain, bias, expand, bias_expand, reduce_w, bias_reduce, scale):
    half = TAPS // 2
    height, width, share = stream.shape
    positions = height * width
    padded = with_halo(stream, (("space", 0),), half)
    padded = jnp.pad(padded.astype(jnp.float32), ((0, 0), (half, half), (0, 0)))
    filtered = jnp.zeros(stream.shape, jnp.float32)
    for row_tap in range(TAPS):
        for col_tap in range(TAPS):
            filtered = filtered + padded[
                row_tap : row_tap + height, col_tap : col_tap + width
            ] * kernel[row_tap, col_tap].astype(jnp.float32)
    filtered = filtered.reshape(positions, share)
    offset = lax.axis_index("tensor") * share
    gain_part = lax.dynamic_slice_in_dim(gain, offset, share, 0)
    bias_part = lax.dynamic_slice_in_dim(bias, offset, share, 0)
    sums, squares = lax.psum(
        (jnp.sum(filtered, axis=-1), jnp.sum(filtered * filtered, axis=-1)), "tensor"
    )
    mean = (sums / D)[:, None]
    var = jnp.maximum(squares[:, None] / D - mean * mean, 0.0)
    normed_part = ((filtered - mean) / jnp.sqrt(var + 1e-06) * gain_part + bias_part).astype(
        jnp.bfloat16
    )
    preact = jnp.dot(
        lax.all_gather(normed_part, "tensor", axis=1, tiled=True),
        expand,
        preferred_element_type=jnp.float32,
    )
    hidden = jax.nn.gelu(preact + bias_expand, approximate=False).astype(jnp.bfloat16)
    partial_value = jnp.dot(hidden, reduce_w, preferred_element_type=jnp.float32)
    mixed = lax.psum_scatter(
        partial_value.astype(jnp.bfloat16), "tensor", scatter_dimension=1, tiled=True
    ).astype(jnp.float32)
    updated = stream.reshape(positions, share).astype(jnp.float32) + scale * (mixed + bias_reduce)
    return updated.astype(jnp.bfloat16).reshape(height, width, share)


def per_device(
    features,
    depth_kernel,
    norm_gain,
    norm_bias,
    w_expand,
    b_expand,
    w_reduce,
    b_reduce,
    layer_scale,
):
    stream = features
    for block_id in range(BLOCKS):
        stream = one_block(
            stream,
            depth_kernel[block_id],
            norm_gain[block_id],
            norm_bias[block_id],
            w_expand[block_id],
            b_expand[block_id],
            w_reduce[block_id],
            b_reduce[block_id],
            layer_scale[block_id],
        )
    return stream


MESH = pl.DeviceIdType.MESH
CORES = 4


def shift_down(x, first):
    return jnp.where(first, 0.0, pltpu.roll(x, 1, 0))


def shift_up(x, last):
    return jnp.where(last, 0.0, pltpu.roll(x, x.shape[0] - 1, 0))


def blocks_kernel(
    n_space, feat_in, taps_in, gain_in, nbias_in, w1_in, b1_in, w2_in, b2_in, scale_in, out,
    feat, taps, gain, nbias, w1, b1, w2, b2, scale, taps32, xf, filt, mid, halo, gathered, centers, normed, hidden,
    pair_out, pair_in, cross_out, cross_in, own,
    w_sem, in_sem, halo_send, halo_recv, ag_send, ag_recv, pair_send, pair_recv, cross_send, cross_recv,
):
    rows, width, share = feat.shape
    half = TAPS // 2
    blocks = w1.shape[0]
    band = lax.axis_index("space")
    me = lax.axis_index("tensor")
    core = lax.rem(me, 2)
    mate = me + 1 - 2 * core
    across = lax.rem(me + 2, CORES)
    diagonal = lax.rem(mate + 2, CORES)
    has_up = band > 0
    has_down = band < n_space - 1

    def weight_copies(b):
        return (
            pltpu.make_async_copy(w1_in.at[b], w1.at[b], w_sem.at[b, 0]),
            pltpu.make_async_copy(w2_in.at[b], w2.at[b], w_sem.at[b, 1]),
        )

    pairs_in = (
        (feat_in, feat), (taps_in, taps), (gain_in, gain), (nbias_in, nbias),
        (b1_in, b1), (b2_in, b2), (scale_in, scale),
    )
    small_copies = [
        pltpu.make_async_copy(src, dst, in_sem.at[i]) for i, (src, dst) in enumerate(pairs_in)
    ]
    for copy in small_copies:
        copy.start()
    for b in range(blocks):
        for copy in weight_copies(b):
            copy.start()

    barrier = pltpu.get_barrier_semaphore()
    for who in (mate, across):
        pl.semaphore_signal(barrier, inc=1, device_id=(band, who), device_id_type=MESH)

    @pl.when(has_up)
    def _():
        pl.semaphore_signal(barrier, inc=1, device_id=(band - 1, me), device_id_type=MESH)

    @pl.when(has_down)
    def _():
        pl.semaphore_signal(barrier, inc=1, device_id=(band + 1, me), device_id_type=MESH)

    pl.semaphore_wait(barrier, 2 + jnp.minimum(band, 1) + jnp.minimum(n_space - 1 - band, 1))

    def remote(src, dst, send, recv, who):
        return pltpu.make_async_remote_copy(
            src_ref=src, dst_ref=dst, send_sem=send, recv_sem=recv, device_id=who, device_id_type=MESH
        )

    def halo_copy(b, source, side, i):
        row = i if side == 0 else rows - half + i
        target = (band - 1, me) if side == 0 else (band + 1, me)
        return remote(
            source.at[row], halo.at[b, side, i], halo_send.at[b, side, i], halo_recv.at[b, side, i], target
        )

    present = (has_up, has_down)

    def ag_copy(b, r, kind):
        slot, target = ((me, mate), (me, across), (across, mate))[kind % 3]
        ref = (gathered if kind < 3 else centers).at[b, r, slot]
        return remote(ref, ref, ag_send.at[b, r, kind], ag_recv.at[b, r, kind], (band, target))

    def pair_copy(b, r):
        return remote(
            pair_out.at[b, r], pair_in.at[b, r], pair_send.at[b, r], pair_recv.at[b, r], (band, mate)
        )

    def cross_copy(b, r):
        return remote(
            cross_out.at[b, r], cross_in.at[b, r], cross_send.at[b, r], cross_recv.at[b, r], (band, across)
        )

    column = lax.broadcasted_iota(jnp.int32, (width, 128), 0)
    lane = lax.broadcasted_iota(jnp.int32, (width, 128), 1)
    first, last, diag = column == 0, column == width - 1, column == lane

    def convolve(b, r, pairs):
        def part(h, fresh):
            ch = pl.ds(pl.multiple_of(h * 128, 128), 128)

            def along(j):
                total = None
                for row, tap in pairs:
                    term = xf[row, :, ch] * taps32[b, tap, pl.ds(j, 1), ch]
                    total = term if total is None else total + term
                return total

            right = shift_down(along(0), first)
            for j in range(1, half):
                right = shift_down(right + along(j), first)
            left = shift_up(along(TAPS - 1), last)
            for j in range(TAPS - 2, half, -1):
                left = shift_up(left + along(j), last)
            total = along(half) + right + left
            if not fresh:
                total = total + filt[r, :, ch]
            filt[r, :, ch] = total

        return part

    def early_rows(b):
        if b == 0:
            return range(rows)
        return range(rows - 1) if b % 2 == 1 else range(1, rows)

    def conv_own(b):
        def body(step, carry):
            r, h = step // (share // 128), lax.rem(step, share // 128)
            convolve(b, r, [(half + m, half + m - r) for m in early_rows(b)])(h, True)
            return carry

        lax.fori_loop(0, rows * (share // 128), body, 0)

    def conv_halo(b, r):
        pairs = [(half + m, half + m - r) for m in range(rows) if m not in early_rows(b)]
        for m in range(half):
            row = r + m + rows * ((r + m) // half)
            pairs.append((row, row - r))

        def body(h, carry):
            convolve(b, r, pairs)(h, False)
            return carry

        lax.fori_loop(0, share // 128, body, 0)

    def take_halo(b, upper, i):
        side, base, there = (1, 0, has_up) if upper else (0, half + rows, has_down)

        @pl.when(there)
        def _():
            halo_copy(b, mid, side, i).wait_recv()
            xf[base + i] = halo[b, side, i].astype(jnp.float32)

        @pl.when(jnp.logical_not(there))
        def _():
            xf[base + i] = jnp.zeros((width, share), jnp.float32)

    def send_filtered(b, r):
        value = filt[r]
        center = jnp.sum(value, axis=1, keepdims=True) / share
        gathered[b, r, me] = (value - center).astype(jnp.bfloat16)
        centers[b, r, me] = jnp.sum(jnp.where(diag, center, 0.0), axis=0, keepdims=True)
        for kind in (4, 1, 3, 0):
            ag_copy(b, r, kind).start()

    def normalize(b, r):
        own_means = [
            jnp.sum(jnp.where(diag, centers[b, r, s], 0.0), axis=1, keepdims=True) for s in range(CORES)
        ]
        mean = (own_means[0] + own_means[1] + own_means[2] + own_means[3]) / CORES
        deltas = [c - mean for c in own_means]
        squares = jnp.zeros((width, 1), jnp.float32)
        for s in range(CORES):
            value = gathered[b, r, s].astype(jnp.float32) + deltas[s]
            squares = squares + jnp.sum(value * value, axis=1, keepdims=True)
        inverse = lax.rsqrt(squares / (share * CORES) + 1e-06)
        for s in range(CORES):
            ch = pl.ds(s * share, share)
            value = gathered[b, r, s].astype(jnp.float32) + deltas[s]
            value = value * inverse * gain[pl.ds(b, 1), ch] + nbias[pl.ds(b, 1), ch]
            normed[:, ch] = value.astype(jnp.bfloat16)

    def expand(b):
        for n in range(w1.shape[2] // 256):
            ch = pl.ds(n * 256, 256)
            x = jnp.dot(normed[...], w1[b, :, ch], preferred_element_type=jnp.float32) + b1[pl.ds(b, 1), ch]
            hidden[:, ch] = (0.5 * x * (1.0 + lax.erf(x * 0.7071067811865476))).astype(jnp.bfloat16)

    def reduce_to(b, owner):
        ch = pl.ds(pl.multiple_of(owner * share, share), share)
        return jnp.dot(hidden[...], w2[b, :, ch], preferred_element_type=jnp.float32)

    def pair_sum(b, r):
        pair_copy(b, r).wait_recv()
        total = cross_out[b, r].astype(jnp.float32) + pair_in[b, r, 1].astype(jnp.float32)
        cross_out[b, r] = total.astype(jnp.bfloat16)
        cross_copy(b, r).start()

    def finish(b, r):
        cross_copy(b, r).wait_recv()
        mixed = own[r] + pair_in[b, r, 0].astype(jnp.float32) + cross_in[b, r].astype(jnp.float32)
        before = (feat if b == 0 else mid)[r].astype(jnp.float32)
        new = (before + scale[pl.ds(b, 1), :] * (mixed + b2[pl.ds(b, 1), :])).astype(jnp.bfloat16)
        if b == blocks - 1:
            out[r] = new
            return
        mid[r] = new
        xf[half + r] = new.astype(jnp.float32)

    def send_halo(b, source, side, i):
        @pl.when(present[side])
        def _():
            halo_copy(b, source, side, i).start()

    for i in range(half):
        send_halo(0, feat_in, 1, i)
    for copy in small_copies:
        copy.wait()
    for b in range(blocks):
        taps32[b] = taps[:, :, b, :].astype(jnp.float32)
    for r in range(rows):
        xf[half + r] = feat[r].astype(jnp.float32)

    for b in range(blocks):
        downward = b % 2 == 0
        row_of = (lambda k: k) if downward else (lambda k: rows - 1 - k)
        if b == 0:
            conv_own(b)

            @pl.when(has_down)
            def _():
                for i in range(half):
                    halo_copy(0, feat_in, 1, i).wait_send()

            for i in range(half):
                send_halo(0, feat_in, 0, i)
        else:
            send_halo(b, mid, 1 if not downward else 0, half - 2 if not downward else 1)

        for i in range(half):
            take_halo(b, downward, i)

        def front(k, carry, b=b, row_of=row_of, downward=downward):
            r = row_of(k)

            @pl.when(k > 0)
            def _():
                take_halo(b, not downward, k - 1 if downward else rows - 1 - k)

            conv_halo(b, r)
            send_filtered(b, r)
            return carry

        if b > 0:
            front(0, 0)
            send_halo(b, mid, 1 if not downward else 0, 0 if not downward else half - 1)
            lax.fori_loop(1, rows, front, 0)
        else:
            lax.fori_loop(0, rows, front, 0)
        for copy in weight_copies(b):
            copy.wait()

        def relay(r, b=b):
            for kind in (4, 1):
                ag_copy(b, r, kind).wait_recv()
                ag_copy(b, r, kind + 1).start()

        def arrive(r, b=b):
            for kind in (0, 3, 2, 5):
                ag_copy(b, r, kind).wait_recv()

        def send_partials(r, b=b):
            pair_out[b, r, 0] = reduce_to(b, mate).astype(jnp.bfloat16)
            pair_out[b, r, 1] = reduce_to(b, diagonal).astype(jnp.bfloat16)
            pair_copy(b, r).start()

        def keep_partials(r, b=b):
            own[r] = reduce_to(b, me)
            cross_out[b, r] = reduce_to(b, across).astype(jnp.bfloat16)

        def finish_and_send(k, b=b, row_of=row_of, downward=downward):
            r = row_of(k)
            finish(b, r)
            if b < blocks - 1:
                send_halo(b + 1, mid, 0 if downward else 1, r if downward else r - (rows - half))

        relay(row_of(0))
        arrive(row_of(0))
        normalize(b, row_of(0))

        def middle(k, carry, b=b, row_of=row_of):
            r = row_of(k)
            after = row_of(k + 1)
            expand(b)
            relay(after)

            @pl.when(k > 0)
            def _():
                pair_sum(b, row_of(k - 1))

            send_partials(r)
            arrive(after)
            keep_partials(r)
            normalize(b, after)

            @pl.when(k > 1)
            def _():
                finish_and_send(k - 2)

            return carry

        lax.fori_loop(0, rows - 1, middle, 0)
        expand(b)
        pair_sum(b, row_of(rows - 2))
        send_partials(row_of(rows - 1))
        keep_partials(row_of(rows - 1))
        finish_and_send(rows - 3)
        pair_sum(b, row_of(rows - 1))
        finish_and_send(rows - 2)
        if b < blocks - 1:
            conv_own(b + 1)
        finish(b, row_of(rows - 1))
        if b < blocks - 1:
            send_halo(b + 1, mid, 1 if downward else 0, half - 1 if downward else 0)

    for b in range(blocks):
        for side in range(2):
            if b == 0 and side == 1:
                continue

            @pl.when(present[side])
            def _(b=b, side=side):
                for i in range(half):
                    halo_copy(b, feat_in if b == 0 else mid, side, i).wait_send()

        def drain(r, carry, b=b):
            for kind in range(6):
                ag_copy(b, r, kind).wait_send()
            pair_copy(b, r).wait_send()
            cross_copy(b, r).wait_send()
            return carry

        lax.fori_loop(0, rows, drain, 0)


def fused(n_space, features, depth_kernel, gain, nbias, w1, b1, w2, b2, scale):
    rows, width, share = features.shape
    blocks, depth, units = w1.shape
    half = TAPS // 2
    depth_kernel = jnp.transpose(depth_kernel, (1, 2, 0, 3))
    operands = (features, depth_kernel, gain, nbias, w1, b1, w2, b2, scale)
    vmem = pl.BlockSpec(memory_space=pltpu.VMEM)
    hbm = pl.BlockSpec(memory_space=pl.ANY)
    bf, f32 = jnp.bfloat16, jnp.float32
    dma = pltpu.SemaphoreType.DMA
    return pl.pallas_call(
        functools.partial(blocks_kernel, n_space),
        out_shape=jax.ShapeDtypeStruct(features.shape, bf),
        in_specs=[hbm] * len(operands),
        out_specs=vmem,
        scratch_shapes=[
            *[pltpu.VMEM(a.shape, a.dtype) for a in operands],
            pltpu.VMEM((blocks, TAPS, TAPS, share), f32),
            pltpu.VMEM((rows + 2 * half, width, share), f32),
            pltpu.VMEM((rows, width, share), f32),
            pltpu.VMEM((rows, width, share), bf),
            pltpu.VMEM((blocks, 2, half, width, share), bf),
            pltpu.VMEM((blocks, rows, CORES, width, share), bf),
            pltpu.VMEM((blocks, rows, CORES, 1, width), f32),
            pltpu.VMEM((width, depth), bf),
            pltpu.VMEM((width, units), bf),
            pltpu.VMEM((blocks, rows, 2, width, share), bf),
            pltpu.VMEM((blocks, rows, 2, width, share), bf),
            pltpu.VMEM((blocks, rows, width, share), bf),
            pltpu.VMEM((blocks, rows, width, share), bf),
            pltpu.VMEM((rows, width, share), f32),
            dma((blocks, 2)),
            dma((7,)),
            dma((blocks, 2, half)),
            dma((blocks, 2, half)),
            dma((blocks, rows, 6)),
            dma((blocks, rows, 6)),
            dma((blocks, rows)),
            dma((blocks, rows)),
            dma((blocks, rows)),
            dma((blocks, rows)),
        ],
        compiler_params=pltpu.CompilerParams(
            collective_id=0, has_side_effects=True, vmem_limit_bytes=64 * 1024 * 1024
        ),
    )(*operands)


def solution(mesh):
    sizes = dict(mesh.shape)

    def body(features, *rest):
        if sizes["tensor"] == CORES and features.shape == (TAPS // 2 + 1, 128, 256):
            return fused(sizes["space"], features, *rest)
        return per_device(features, *rest)

    return jax.shard_map(
        body,
        mesh=mesh,
        in_specs=(
            P("space", None, "tensor"),
            P(None, None, None, "tensor"),
            P(),
            P(),
            P(None, None, "tensor"),
            P(None, "tensor"),
            P(None, "tensor", None),
            P(None, "tensor"),
            P(None, "tensor"),
        ),
        out_specs=P("space", None, "tensor"),
        check_vma=False,
    )
```

```python
import functools

import jax
import jax.numpy as jnp
from jax import lax
from jax.experimental import pallas as pl
from jax.experimental.pallas import tpu as pltpu
from jax.sharding import PartitionSpec as P

D = 1024
TAPS = 7
BLOCKS = 2


def with_halo(x, sides, width):
    for axis, dim in sides:
        devices, length = (lax.axis_size(axis), x.shape[dim])
        up = [(i, (i + 1) % devices) for i in range(devices - 1)]
        down = [(j, i) for i, j in up]
        last = lax.slice_in_dim(x, length - width, length, axis=dim)
        leading = lax.slice_in_dim(x, 0, width, axis=dim)
        before = lax.ppermute(last, axis, up)
        after = lax.ppermute(leading, axis, down)
        x = jnp.concatenate([before, x, after], axis=dim)
    return x


def one_block(stream, kernel, gain, bias, expand, bias_expand, reduce_w, bias_reduce, scale):
    half = TAPS // 2
    height, width, share = stream.shape
    positions = height * width
    padded = with_halo(stream, (("space", 0),), half)
    padded = jnp.pad(padded.astype(jnp.float32), ((0, 0), (half, half), (0, 0)))
    filtered = jnp.zeros(stream.shape, jnp.float32)
    for row_tap in range(TAPS):
        for col_tap in range(TAPS):
            filtered = filtered + padded[
                row_tap : row_tap + height, col_tap : col_tap + width
            ] * kernel[row_tap, col_tap].astype(jnp.float32)
    filtered = filtered.reshape(positions, share)
    offset = lax.axis_index("tensor") * share
    gain_part = lax.dynamic_slice_in_dim(gain, offset, share, 0)
    bias_part = lax.dynamic_slice_in_dim(bias, offset, share, 0)
    sums, squares = lax.psum(
        (jnp.sum(filtered, axis=-1), jnp.sum(filtered * filtered, axis=-1)), "tensor"
    )
    mean = (sums / D)[:, None]
    var = jnp.maximum(squares[:, None] / D - mean * mean, 0.0)
    normed_part = ((filtered - mean) / jnp.sqrt(var + 1e-06) * gain_part + bias_part).astype(
        jnp.bfloat16
    )
    preact = jnp.dot(
        lax.all_gather(normed_part, "tensor", axis=1, tiled=True),
        expand,
        preferred_element_type=jnp.float32,
    )
    hidden = jax.nn.gelu(preact + bias_expand, approximate=False).astype(jnp.bfloat16)
    partial_value = jnp.dot(hidden, reduce_w, preferred_element_type=jnp.float32)
    mixed = lax.psum_scatter(
        partial_value.astype(jnp.bfloat16), "tensor", scatter_dimension=1, tiled=True
    ).astype(jnp.float32)
    updated = stream.reshape(positions, share).astype(jnp.float32) + scale * (mixed + bias_reduce)
    return updated.astype(jnp.bfloat16).reshape(height, width, share)


def per_device(
    features,
    depth_kernel,
    norm_gain,
    norm_bias,
    w_expand,
    b_expand,
    w_reduce,
    b_reduce,
    layer_scale,
):
    stream = features
    for block_id in range(BLOCKS):
        stream = one_block(
            stream,
            depth_kernel[block_id],
            norm_gain[block_id],
            norm_bias[block_id],
            w_expand[block_id],
            b_expand[block_id],
            w_reduce[block_id],
            b_reduce[block_id],
            layer_scale[block_id],
        )
    return stream


MESH = pl.DeviceIdType.MESH
CORES = 4


def shift_down(x, first):
    return jnp.where(first, 0.0, pltpu.roll(x, 1, 0))


def shift_up(x, last):
    return jnp.where(last, 0.0, pltpu.roll(x, x.shape[0] - 1, 0))


ERFC_P = 0.3275911
ERFC_A = (0.254829592, -0.284496736, 1.421413741, -1.453152027, 1.061405429)


def gelu(x):
    size = jnp.abs(x)
    t = 1.0 / (1.0 + (ERFC_P * 0.5**0.5) * size)
    series = 0.5 * ERFC_A[4]
    for a in ERFC_A[3::-1]:
        series = series * t + 0.5 * a
    tail = series * t * jnp.exp(-0.5 * (x * x))
    return jnp.maximum(x, 0.0) - size * tail


def blocks_kernel(
    n_space, feat_in, taps_in, gain_in, nbias_in, w1_in, b1_in, w2_in, b2_in, scale_in, out,
    feat, taps, gain, nbias, w1, b1, w2, b2, scale, taps32, xf, filt, mid, halo, gathered, centers, normed, hidden,
    pair_out, pair_in, cross_out, cross_in, own,
    w_sem, in_sem, halo_send, halo_recv, ag_send, ag_recv, pair_send, pair_recv, cross_send, cross_recv,
):
    rows, width, share = feat.shape
    half = TAPS // 2
    blocks = w1.shape[0]
    band = lax.axis_index("space")
    me = lax.axis_index("tensor")
    core = lax.rem(me, 2)
    mate = me + 1 - 2 * core
    across = lax.rem(me + 2, CORES)
    diagonal = lax.rem(mate + 2, CORES)
    has_up = band > 0
    has_down = band < n_space - 1

    def weight_copies(b):
        return (
            pltpu.make_async_copy(w1_in.at[b], w1.at[b], w_sem.at[b, 0]),
            pltpu.make_async_copy(w2_in.at[b], w2.at[b], w_sem.at[b, 1]),
        )

    pairs_in = (
        (feat_in, feat), (taps_in, taps), (gain_in, gain), (nbias_in, nbias),
        (b1_in, b1), (b2_in, b2), (scale_in, scale),
    )
    small_copies = [
        pltpu.make_async_copy(src, dst, in_sem.at[i]) for i, (src, dst) in enumerate(pairs_in)
    ]
    for copy in small_copies:
        copy.start()
    for b in range(blocks):
        for copy in weight_copies(b):
            copy.start()

    barrier = pltpu.get_barrier_semaphore()
    for who in (mate, across):
        pl.semaphore_signal(barrier, inc=1, device_id=(band, who), device_id_type=MESH)

    @pl.when(has_up)
    def _():
        pl.semaphore_signal(barrier, inc=1, device_id=(band - 1, me), device_id_type=MESH)

    @pl.when(has_down)
    def _():
        pl.semaphore_signal(barrier, inc=1, device_id=(band + 1, me), device_id_type=MESH)

    pl.semaphore_wait(barrier, 2 + jnp.minimum(band, 1) + jnp.minimum(n_space - 1 - band, 1))

    def remote(src, dst, send, recv, who):
        return pltpu.make_async_remote_copy(
            src_ref=src, dst_ref=dst, send_sem=send, recv_sem=recv, device_id=who, device_id_type=MESH
        )

    def halo_copy(b, source, side, i):
        row = i if side == 0 else rows - half + i
        target = (band - 1, me) if side == 0 else (band + 1, me)
        return remote(
            source.at[row], halo.at[b, side, i], halo_send.at[b, side, i], halo_recv.at[b, side, i], target
        )

    present = (has_up, has_down)

    def ag_copy(b, r, kind):
        slot, target = ((me, mate), (me, across), (across, mate))[kind % 3]
        ref = (gathered if kind < 3 else centers).at[b, r, slot]
        return remote(ref, ref, ag_send.at[b, r, kind], ag_recv.at[b, r, kind], (band, target))

    def pair_copy(b, r):
        return remote(
            pair_out.at[b, r], pair_in.at[b, r], pair_send.at[b, r], pair_recv.at[b, r], (band, mate)
        )

    def cross_copy(b, r):
        return remote(
            cross_out.at[b, r], cross_in.at[b, r], cross_send.at[b, r], cross_recv.at[b, r], (band, across)
        )

    column = lax.broadcasted_iota(jnp.int32, (width, 128), 0)
    lane = lax.broadcasted_iota(jnp.int32, (width, 128), 1)
    first, last, diag = column == 0, column == width - 1, column == lane

    def convolve(b, r, pairs):
        def part(h, fresh):
            ch = pl.ds(pl.multiple_of(h * 128, 128), 128)

            def along(j):
                total = None
                for row, tap in pairs:
                    term = xf[row, :, ch] * taps32[b, tap, pl.ds(j, 1), ch]
                    total = term if total is None else total + term
                return total

            right = shift_down(along(0), first)
            for j in range(1, half):
                right = shift_down(right + along(j), first)
            left = shift_up(along(TAPS - 1), last)
            for j in range(TAPS - 2, half, -1):
                left = shift_up(left + along(j), last)
            total = along(half) + right + left
            if not fresh:
                total = total + filt[r, :, ch]
            filt[r, :, ch] = total

        return part

    def early_rows(b):
        if b == 0:
            return range(rows)
        return range(rows - 1) if b % 2 == 1 else range(1, rows)

    def conv_own(b):
        def body(step, carry):
            r, h = step // (share // 128), lax.rem(step, share // 128)
            convolve(b, r, [(half + m, half + m - r) for m in early_rows(b)])(h, True)
            return carry

        lax.fori_loop(0, rows * (share // 128), body, 0)

    def conv_halo(b, r):
        pairs = [(half + m, half + m - r) for m in range(rows) if m not in early_rows(b)]
        for m in range(half):
            row = r + m + rows * ((r + m) // half)
            pairs.append((row, row - r))

        def body(h, carry):
            convolve(b, r, pairs)(h, False)
            return carry

        lax.fori_loop(0, share // 128, body, 0)

    def take_halo(b, upper, i):
        side, base, there = (1, 0, has_up) if upper else (0, half + rows, has_down)

        @pl.when(there)
        def _():
            halo_copy(b, mid, side, i).wait_recv()
            xf[base + i] = halo[b, side, i].astype(jnp.float32)

        @pl.when(jnp.logical_not(there))
        def _():
            xf[base + i] = jnp.zeros((width, share), jnp.float32)

    def send_filtered(b, r):
        value = filt[r]
        center = jnp.sum(value, axis=1, keepdims=True) / share
        gathered[b, r, me] = (value - center).astype(jnp.bfloat16)
        centers[b, r, me] = jnp.sum(jnp.where(diag, center, 0.0), axis=0, keepdims=True)
        for kind in (4, 1, 3, 0):
            ag_copy(b, r, kind).start()

    def normalize(b, r):
        own_means = [
            jnp.sum(jnp.where(diag, centers[b, r, s], 0.0), axis=1, keepdims=True) for s in range(CORES)
        ]
        mean = (own_means[0] + own_means[1] + own_means[2] + own_means[3]) / CORES
        deltas = [c - mean for c in own_means]
        squares = jnp.zeros((width, share), jnp.float32)
        for s in range(CORES):
            value = gathered[b, r, s].astype(jnp.float32) + deltas[s]
            squares = squares + value * value
        var = jnp.sum(squares, axis=1, keepdims=True) / (share * CORES)
        inverse = lax.rsqrt(var + 1e-06)
        for s in range(CORES):
            ch = pl.ds(s * share, share)
            value = gathered[b, r, s].astype(jnp.float32) + deltas[s]
            value = value * inverse * gain[pl.ds(b, 1), ch] + nbias[pl.ds(b, 1), ch]
            normed[:, ch] = value.astype(jnp.bfloat16)

    def expand(b):
        for n in range(w1.shape[2] // 256):
            ch = pl.ds(n * 256, 256)
            x = jnp.dot(normed[...], w1[b, :, ch], preferred_element_type=jnp.float32) + b1[pl.ds(b, 1), ch]
            hidden[:, ch] = gelu(x).astype(jnp.bfloat16)

    def reduce_to(b, owner):
        ch = pl.ds(pl.multiple_of(owner * share, share), share)
        return jnp.dot(hidden[...], w2[b, :, ch], preferred_element_type=jnp.float32)

    def pair_sum(b, r):
        pair_copy(b, r).wait_recv()
        total = cross_out[b, r].astype(jnp.float32) + pair_in[b, r, 1].astype(jnp.float32)
        cross_out[b, r] = total.astype(jnp.bfloat16)
        cross_copy(b, r).start()

    def finish(b, r):
        cross_copy(b, r).wait_recv()
        mixed = own[r] + pair_in[b, r, 0].astype(jnp.float32) + cross_in[b, r].astype(jnp.float32)
        before = (feat if b == 0 else mid)[r].astype(jnp.float32)
        new = (before + scale[pl.ds(b, 1), :] * (mixed + b2[pl.ds(b, 1), :])).astype(jnp.bfloat16)
        if b == blocks - 1:
            out[r] = new
            return
        mid[r] = new
        xf[half + r] = new.astype(jnp.float32)

    def send_halo(b, source, side, i):
        @pl.when(present[side])
        def _():
            halo_copy(b, source, side, i).start()

    for i in range(half):
        send_halo(0, feat_in, 1, i)
    for copy in small_copies:
        copy.wait()
    for b in range(blocks):
        taps32[b] = taps[:, :, b, :].astype(jnp.float32)
    for r in range(rows):
        xf[half + r] = feat[r].astype(jnp.float32)

    for b in range(blocks):
        downward = b % 2 == 0
        row_of = (lambda k: k) if downward else (lambda k: rows - 1 - k)
        if b == 0:
            conv_own(b)

            @pl.when(has_down)
            def _():
                for i in range(half):
                    halo_copy(0, feat_in, 1, i).wait_send()

            for i in range(half):
                send_halo(0, feat_in, 0, i)
        else:
            send_halo(b, mid, 1 if not downward else 0, half - 2 if not downward else 1)

        for i in range(half):
            take_halo(b, downward, i)

        def front(k, carry, b=b, row_of=row_of, downward=downward):
            r = row_of(k)

            @pl.when(k > 0)
            def _():
                take_halo(b, not downward, k - 1 if downward else rows - 1 - k)

            conv_halo(b, r)
            send_filtered(b, r)
            return carry

        if b > 0:
            front(0, 0)
            send_halo(b, mid, 1 if not downward else 0, 0 if not downward else half - 1)
            lax.fori_loop(1, rows, front, 0)
        else:
            lax.fori_loop(0, rows, front, 0)
        for copy in weight_copies(b):
            copy.wait()

        def relay(r, b=b):
            for kind in (4, 1):
                ag_copy(b, r, kind).wait_recv()
                ag_copy(b, r, kind + 1).start()

        def arrive(r, b=b):
            for kind in (0, 3, 2, 5):
                ag_copy(b, r, kind).wait_recv()

        def send_partials(r, b=b):
            pair_out[b, r, 0] = reduce_to(b, mate).astype(jnp.bfloat16)
            pair_out[b, r, 1] = reduce_to(b, diagonal).astype(jnp.bfloat16)
            pair_copy(b, r).start()

        def keep_partials(r, b=b):
            own[r] = reduce_to(b, me)
            cross_out[b, r] = reduce_to(b, across).astype(jnp.bfloat16)

        def finish_and_send(k, b=b, row_of=row_of, downward=downward):
            r = row_of(k)
            finish(b, r)
            if b < blocks - 1:
                send_halo(b + 1, mid, 0 if downward else 1, r if downward else r - (rows - half))

        relay(row_of(0))
        arrive(row_of(0))
        normalize(b, row_of(0))

        def middle(k, carry, b=b, row_of=row_of):
            r = row_of(k)
            after = row_of(k + 1)
            expand(b)
            relay(after)

            @pl.when(k > 0)
            def _():
                pair_sum(b, row_of(k - 1))

            send_partials(r)
            arrive(after)
            keep_partials(r)
            normalize(b, after)

            @pl.when(k > 1)
            def _():
                finish_and_send(k - 2)

            return carry

        lax.fori_loop(0, rows - 1, middle, 0)
        expand(b)
        pair_sum(b, row_of(rows - 2))
        send_partials(row_of(rows - 1))
        keep_partials(row_of(rows - 1))
        finish_and_send(rows - 3)
        pair_sum(b, row_of(rows - 1))
        finish_and_send(rows - 2)
        if b < blocks - 1:
            conv_own(b + 1)
        finish(b, row_of(rows - 1))
        if b < blocks - 1:
            send_halo(b + 1, mid, 1 if downward else 0, half - 1 if downward else 0)

    for b in range(blocks):
        for side in range(2):
            if b == 0 and side == 1:
                continue

            @pl.when(present[side])
            def _(b=b, side=side):
                for i in range(half):
                    halo_copy(b, feat_in if b == 0 else mid, side, i).wait_send()

        def drain(r, carry, b=b):
            for kind in range(6):
                ag_copy(b, r, kind).wait_send()
            pair_copy(b, r).wait_send()
            cross_copy(b, r).wait_send()
            return carry

        lax.fori_loop(0, rows, drain, 0)


def fused(n_space, features, depth_kernel, gain, nbias, w1, b1, w2, b2, scale):
    rows, width, share = features.shape
    blocks, depth, units = w1.shape
    half = TAPS // 2
    depth_kernel = jnp.transpose(depth_kernel, (1, 2, 0, 3))
    operands = (features, depth_kernel, gain, nbias, w1, b1, w2, b2, scale)
    vmem = pl.BlockSpec(memory_space=pltpu.VMEM)
    hbm = pl.BlockSpec(memory_space=pl.ANY)
    bf, f32 = jnp.bfloat16, jnp.float32
    dma = pltpu.SemaphoreType.DMA
    return pl.pallas_call(
        functools.partial(blocks_kernel, n_space),
        out_shape=jax.ShapeDtypeStruct(features.shape, bf),
        in_specs=[hbm] * len(operands),
        out_specs=vmem,
        scratch_shapes=[
            *[pltpu.VMEM(a.shape, a.dtype) for a in operands],
            pltpu.VMEM((blocks, TAPS, TAPS, share), f32),
            pltpu.VMEM((rows + 2 * half, width, share), f32),
            pltpu.VMEM((rows, width, share), f32),
            pltpu.VMEM((rows, width, share), bf),
            pltpu.VMEM((blocks, 2, half, width, share), bf),
            pltpu.VMEM((blocks, rows, CORES, width, share), bf),
            pltpu.VMEM((blocks, rows, CORES, 1, width), f32),
            pltpu.VMEM((width, depth), bf),
            pltpu.VMEM((width, units), bf),
            pltpu.VMEM((blocks, rows, 2, width, share), bf),
            pltpu.VMEM((blocks, rows, 2, width, share), bf),
            pltpu.VMEM((blocks, rows, width, share), bf),
            pltpu.VMEM((blocks, rows, width, share), bf),
            pltpu.VMEM((rows, width, share), f32),
            dma((blocks, 2)),
            dma((7,)),
            dma((blocks, 2, half)),
            dma((blocks, 2, half)),
            dma((blocks, rows, 6)),
            dma((blocks, rows, 6)),
            dma((blocks, rows)),
            dma((blocks, rows)),
            dma((blocks, rows)),
            dma((blocks, rows)),
        ],
        compiler_params=pltpu.CompilerParams(
            collective_id=0, has_side_effects=True, vmem_limit_bytes=64 * 1024 * 1024
        ),
    )(*operands)


def solution(mesh):
    sizes = dict(mesh.shape)

    def body(features, *rest):
        if sizes["tensor"] == CORES and features.shape == (TAPS // 2 + 1, 128, 256):
            return fused(sizes["space"], features, *rest)
        return per_device(features, *rest)

    return jax.shard_map(
        body,
        mesh=mesh,
        in_specs=(
            P("space", None, "tensor"),
            P(None, None, None, "tensor"),
            P(),
            P(),
            P(None, None, "tensor"),
            P(None, "tensor"),
            P(None, "tensor", None),
            P(None, "tensor"),
            P(None, "tensor"),
        ),
        out_specs=P("space", None, "tensor"),
        check_vma=False,
    )
```

```python
import functools

import jax
import jax.numpy as jnp
from jax import lax
from jax.experimental import pallas as pl
from jax.experimental.pallas import tpu as pltpu
from jax.sharding import PartitionSpec as P

D = 1024
TAPS = 7
BLOCKS = 2


def with_halo(x, sides, width):
    for axis, dim in sides:
        devices, length = (lax.axis_size(axis), x.shape[dim])
        up = [(i, (i + 1) % devices) for i in range(devices - 1)]
        down = [(j, i) for i, j in up]
        last = lax.slice_in_dim(x, length - width, length, axis=dim)
        leading = lax.slice_in_dim(x, 0, width, axis=dim)
        before = lax.ppermute(last, axis, up)
        after = lax.ppermute(leading, axis, down)
        x = jnp.concatenate([before, x, after], axis=dim)
    return x


def one_block(stream, kernel, gain, bias, expand, bias_expand, reduce_w, bias_reduce, scale):
    half = TAPS // 2
    height, width, share = stream.shape
    positions = height * width
    padded = with_halo(stream, (("space", 0),), half)
    padded = jnp.pad(padded.astype(jnp.float32), ((0, 0), (half, half), (0, 0)))
    filtered = jnp.zeros(stream.shape, jnp.float32)
    for row_tap in range(TAPS):
        for col_tap in range(TAPS):
            filtered = filtered + padded[
                row_tap : row_tap + height, col_tap : col_tap + width
            ] * kernel[row_tap, col_tap].astype(jnp.float32)
    filtered = filtered.reshape(positions, share)
    offset = lax.axis_index("tensor") * share
    gain_part = lax.dynamic_slice_in_dim(gain, offset, share, 0)
    bias_part = lax.dynamic_slice_in_dim(bias, offset, share, 0)
    sums, squares = lax.psum(
        (jnp.sum(filtered, axis=-1), jnp.sum(filtered * filtered, axis=-1)), "tensor"
    )
    mean = (sums / D)[:, None]
    var = jnp.maximum(squares[:, None] / D - mean * mean, 0.0)
    normed_part = ((filtered - mean) / jnp.sqrt(var + 1e-06) * gain_part + bias_part).astype(
        jnp.bfloat16
    )
    preact = jnp.dot(
        lax.all_gather(normed_part, "tensor", axis=1, tiled=True),
        expand,
        preferred_element_type=jnp.float32,
    )
    hidden = jax.nn.gelu(preact + bias_expand, approximate=False).astype(jnp.bfloat16)
    partial_value = jnp.dot(hidden, reduce_w, preferred_element_type=jnp.float32)
    mixed = lax.psum_scatter(
        partial_value.astype(jnp.bfloat16), "tensor", scatter_dimension=1, tiled=True
    ).astype(jnp.float32)
    updated = stream.reshape(positions, share).astype(jnp.float32) + scale * (mixed + bias_reduce)
    return updated.astype(jnp.bfloat16).reshape(height, width, share)


def per_device(
    features,
    depth_kernel,
    norm_gain,
    norm_bias,
    w_expand,
    b_expand,
    w_reduce,
    b_reduce,
    layer_scale,
):
    stream = features
    for block_id in range(BLOCKS):
        stream = one_block(
            stream,
            depth_kernel[block_id],
            norm_gain[block_id],
            norm_bias[block_id],
            w_expand[block_id],
            b_expand[block_id],
            w_reduce[block_id],
            b_reduce[block_id],
            layer_scale[block_id],
        )
    return stream


MESH = pl.DeviceIdType.MESH
CORES = 4


def shift_down(x, first):
    return jnp.where(first, 0.0, pltpu.roll(x, 1, 0))


def shift_up(x, last):
    return jnp.where(last, 0.0, pltpu.roll(x, x.shape[0] - 1, 0))


def blocks_kernel(
    n_space, feat_in, taps_in, gain_in, nbias_in, w1_in, b1_in, w2_in, b2_in, scale_in, out,
    feat, taps, gain, nbias, w1, b1, w2, b2, scale, taps32, xf, filt, mid, halo, gathered, centers, normed, hidden,
    pair_out, pair_in, cross_out, cross_in, own,
    w_sem, in_sem, halo_send, halo_recv, ag_send, ag_recv, pair_send, pair_recv, cross_send, cross_recv,
):
    rows, width, share = feat.shape
    half = TAPS // 2
    blocks = w1.shape[0]
    band = lax.axis_index("space")
    me = lax.axis_index("tensor")
    core = lax.rem(me, 2)
    mate = me + 1 - 2 * core
    across = lax.rem(me + 2, CORES)
    diagonal = lax.rem(mate + 2, CORES)
    has_up = band > 0
    has_down = band < n_space - 1

    def weight_copies(b):
        return (
            pltpu.make_async_copy(w1_in.at[b], w1.at[b], w_sem.at[b, 0]),
            pltpu.make_async_copy(w2_in.at[b], w2.at[b], w_sem.at[b, 1]),
        )

    pairs_in = (
        (feat_in, feat), (taps_in, taps), (gain_in, gain), (nbias_in, nbias),
        (b1_in, b1), (b2_in, b2), (scale_in, scale),
    )
    small_copies = [
        pltpu.make_async_copy(src, dst, in_sem.at[i]) for i, (src, dst) in enumerate(pairs_in)
    ]
    for copy in small_copies:
        copy.start()
    for b in range(blocks):
        for copy in weight_copies(b):
            copy.start()

    barrier = pltpu.get_barrier_semaphore()
    for who in (mate, across):
        pl.semaphore_signal(barrier, inc=1, device_id=(band, who), device_id_type=MESH)

    @pl.when(has_up)
    def _():
        pl.semaphore_signal(barrier, inc=1, device_id=(band - 1, me), device_id_type=MESH)

    @pl.when(has_down)
    def _():
        pl.semaphore_signal(barrier, inc=1, device_id=(band + 1, me), device_id_type=MESH)

    pl.semaphore_wait(barrier, 2 + jnp.minimum(band, 1) + jnp.minimum(n_space - 1 - band, 1))

    def remote(src, dst, send, recv, who):
        return pltpu.make_async_remote_copy(
            src_ref=src, dst_ref=dst, send_sem=send, recv_sem=recv, device_id=who, device_id_type=MESH
        )

    def halo_copy(b, source, side, i):
        row = i if side == 0 else rows - half + i
        target = (band - 1, me) if side == 0 else (band + 1, me)
        return remote(
            source.at[row], halo.at[b, side, i], halo_send.at[b, side, i], halo_recv.at[b, side, i], target
        )

    present = (has_up, has_down)

    def ag_copy(b, r, kind):
        slot, target = ((me, mate), (me, across), (across, mate))[kind % 3]
        ref = (gathered if kind < 3 else centers).at[b, r, slot]
        return remote(ref, ref, ag_send.at[b, r, kind], ag_recv.at[b, r, kind], (band, target))

    def pair_copy(b, r):
        return remote(
            pair_out.at[b, r], pair_in.at[b, r], pair_send.at[b, r], pair_recv.at[b, r], (band, mate)
        )

    def cross_copy(b, r):
        return remote(
            cross_out.at[b, r], cross_in.at[b, r], cross_send.at[b, r], cross_recv.at[b, r], (band, across)
        )

    column = lax.broadcasted_iota(jnp.int32, (width, 128), 0)
    lane = lax.broadcasted_iota(jnp.int32, (width, 128), 1)
    first, last, diag = column == 0, column == width - 1, column == lane

    def convolve(b, r, pairs):
        def part(h, fresh):
            ch = pl.ds(pl.multiple_of(h * 128, 128), 128)

            def along(j):
                total = None
                for row, tap in pairs:
                    term = xf[row, :, ch] * taps32[b, tap, pl.ds(j, 1), ch]
                    total = term if total is None else total + term
                return total

            right = shift_down(along(0), first)
            for j in range(1, half):
                right = shift_down(right + along(j), first)
            left = shift_up(along(TAPS - 1), last)
            for j in range(TAPS - 2, half, -1):
                left = shift_up(left + along(j), last)
            total = along(half) + right + left
            if not fresh:
                total = total + filt[r, :, ch]
            filt[r, :, ch] = total

        return part

    def early_rows(b):
        if b == 0:
            return range(rows)
        return range(rows - 1) if b % 2 == 1 else range(1, rows)

    def conv_own(b):
        def body(step, carry):
            r, h = step // (share // 128), lax.rem(step, share // 128)
            convolve(b, r, [(half + m, half + m - r) for m in early_rows(b)])(h, True)
            return carry

        lax.fori_loop(0, rows * (share // 128), body, 0)

    def conv_halo(b, r):
        pairs = [(half + m, half + m - r) for m in range(rows) if m not in early_rows(b)]
        for m in range(half):
            row = r + m + rows * ((r + m) // half)
            pairs.append((row, row - r))

        def body(h, carry):
            convolve(b, r, pairs)(h, False)
            return carry

        lax.fori_loop(0, share // 128, body, 0)

    def take_halo(b, upper, i):
        side, base, there = (1, 0, has_up) if upper else (0, half + rows, has_down)

        @pl.when(there)
        def _():
            halo_copy(b, mid, side, i).wait_recv()
            xf[base + i] = halo[b, side, i].astype(jnp.float32)

        @pl.when(jnp.logical_not(there))
        def _():
            xf[base + i] = jnp.zeros((width, share), jnp.float32)

    def send_filtered(b, r):
        value = filt[r]
        center = jnp.sum(value, axis=1, keepdims=True) / share
        gathered[b, r, me] = (value - center).astype(jnp.bfloat16)
        centers[b, r, me] = jnp.sum(jnp.where(diag, center, 0.0), axis=0, keepdims=True)
        for kind in (4, 1, 3, 0):
            ag_copy(b, r, kind).start()

    def normalize(b, r, place):
        own_means = [
            jnp.sum(jnp.where(diag, centers[b, r, s], 0.0), axis=1, keepdims=True) for s in range(CORES)
        ]
        mean = (own_means[0] + own_means[1] + own_means[2] + own_means[3]) / CORES
        deltas = [c - mean for c in own_means]
        squares = jnp.zeros((width, share), jnp.float32)
        for s in range(CORES):
            value = gathered[b, r, s].astype(jnp.float32) + deltas[s]
            squares = squares + value * value
        var = jnp.sum(squares, axis=1, keepdims=True) / (share * CORES)
        inverse = lax.rsqrt(var + 1e-06)
        for s in range(CORES):
            ch = pl.ds(s * share, share)
            value = gathered[b, r, s].astype(jnp.float32) + deltas[s]
            value = value * inverse * gain[pl.ds(b, 1), ch] + nbias[pl.ds(b, 1), ch]
            normed[pl.ds(place * width, width), ch] = value.astype(jnp.bfloat16)

    def expand(b):
        for n in range(w1.shape[2] // 256):
            ch = pl.ds(n * 256, 256)
            x = jnp.dot(normed[...], w1[b, :, ch], preferred_element_type=jnp.float32) + b1[pl.ds(b, 1), ch]
            hidden[:, ch] = (0.5 * x * (1.0 + lax.erf(x * 0.7071067811865476))).astype(jnp.bfloat16)

    def reduce_to(b, owner):
        ch = pl.ds(pl.multiple_of(owner * share, share), share)
        return jnp.dot(hidden[...], w2[b, :, ch], preferred_element_type=jnp.float32)

    def pair_sum(b, r):
        pair_copy(b, r).wait_recv()
        total = cross_out[b, r].astype(jnp.float32) + pair_in[b, r, 1].astype(jnp.float32)
        cross_out[b, r] = total.astype(jnp.bfloat16)
        cross_copy(b, r).start()

    def finish(b, r):
        cross_copy(b, r).wait_recv()
        mixed = own[r] + pair_in[b, r, 0].astype(jnp.float32) + cross_in[b, r].astype(jnp.float32)
        before = (feat if b == 0 else mid)[r].astype(jnp.float32)
        new = (before + scale[pl.ds(b, 1), :] * (mixed + b2[pl.ds(b, 1), :])).astype(jnp.bfloat16)
        if b == blocks - 1:
            out[r] = new
            return
        mid[r] = new
        xf[half + r] = new.astype(jnp.float32)

    def send_halo(b, source, side, i):
        @pl.when(present[side])
        def _():
            halo_copy(b, source, side, i).start()

    for i in range(half):
        send_halo(0, feat_in, 1, i)
    for copy in small_copies:
        copy.wait()
    for b in range(blocks):
        taps32[b] = taps[:, :, b, :].astype(jnp.float32)
    for r in range(rows):
        xf[half + r] = feat[r].astype(jnp.float32)

    for b in range(blocks):
        downward = b % 2 == 0
        row_of = (lambda k: k) if downward else (lambda k: rows - 1 - k)
        if b == 0:
            conv_own(b)

            @pl.when(has_down)
            def _():
                for i in range(half):
                    halo_copy(0, feat_in, 1, i).wait_send()

            for i in range(half):
                send_halo(0, feat_in, 0, i)
        else:
            send_halo(b, mid, 1 if not downward else 0, half - 2 if not downward else 1)

        for i in range(half):
            take_halo(b, downward, i)

        def front(k, carry, b=b, row_of=row_of, downward=downward):
            r = row_of(k)

            @pl.when(k > 0)
            def _():
                take_halo(b, not downward, k - 1 if downward else rows - 1 - k)

            conv_halo(b, r)
            send_filtered(b, r)
            return carry

        if b > 0:
            front(0, 0)
            send_halo(b, mid, 1 if not downward else 0, 0 if not downward else half - 1)
            lax.fori_loop(1, rows, front, 0)
        else:
            lax.fori_loop(0, rows, front, 0)
        for copy in weight_copies(b):
            copy.wait()

        def relay(r, b=b):
            for kind in (4, 1):
                ag_copy(b, r, kind).wait_recv()
                ag_copy(b, r, kind + 1).start()

        def arrive(r, b=b):
            for kind in (0, 3, 2, 5):
                ag_copy(b, r, kind).wait_recv()

        def partials(owner, pair, b=b):
            total = reduce_to(b, owner)
            return [(r, total[i * width : (i + 1) * width]) for i, r in enumerate(pair)]

        def send_partials(pair, b=b):
            for which, owner in enumerate((mate, diagonal)):
                for r, value in partials(owner, pair):
                    pair_out[b, r, which] = value.astype(jnp.bfloat16)
            for r in pair:
                pair_copy(b, r).start()

        def keep_partials(pair, b=b):
            for r, value in partials(across, pair):
                cross_out[b, r] = value.astype(jnp.bfloat16)
            for r, value in partials(me, pair):
                own[r] = value

        def gather_pair(pair, b=b):
            for i, r in enumerate(pair):
                arrive(r)
                normalize(b, r, i)

        def finish_and_send(k, b=b, row_of=row_of, downward=downward):
            r = row_of(k)
            finish(b, r)
            if b < blocks - 1:
                send_halo(b + 1, mid, 0 if downward else 1, r if downward else r - (rows - half))

        early = [row_of(k) for k in range(rows // 2)]
        late = [row_of(k) for k in range(rows // 2, rows)]
        for r in early:
            relay(r)
        gather_pair(early)
        expand(b)
        for r in late:
            relay(r)
        send_partials(early)
        keep_partials(early)
        gather_pair(late)
        for r in early:
            pair_sum(b, r)
        expand(b)
        send_partials(late)
        keep_partials(late)
        for k in range(rows // 2):
            finish_and_send(k)
        for r in late:
            pair_sum(b, r)
        for k in range(rows // 2, rows - 1):
            finish_and_send(k)
        if b < blocks - 1:
            conv_own(b + 1)
        finish(b, row_of(rows - 1))
        if b < blocks - 1:
            send_halo(b + 1, mid, 1 if downward else 0, half - 1 if downward else 0)

    for b in range(blocks):
        for side in range(2):
            if b == 0 and side == 1:
                continue

            @pl.when(present[side])
            def _(b=b, side=side):
                for i in range(half):
                    halo_copy(b, feat_in if b == 0 else mid, side, i).wait_send()

        def drain(r, carry, b=b):
            for kind in range(6):
                ag_copy(b, r, kind).wait_send()
            pair_copy(b, r).wait_send()
            cross_copy(b, r).wait_send()
            return carry

        lax.fori_loop(0, rows, drain, 0)


def fused(n_space, features, depth_kernel, gain, nbias, w1, b1, w2, b2, scale):
    rows, width, share = features.shape
    blocks, depth, units = w1.shape
    half = TAPS // 2
    depth_kernel = jnp.transpose(depth_kernel, (1, 2, 0, 3))
    operands = (features, depth_kernel, gain, nbias, w1, b1, w2, b2, scale)
    vmem = pl.BlockSpec(memory_space=pltpu.VMEM)
    hbm = pl.BlockSpec(memory_space=pl.ANY)
    bf, f32 = jnp.bfloat16, jnp.float32
    dma = pltpu.SemaphoreType.DMA
    return pl.pallas_call(
        functools.partial(blocks_kernel, n_space),
        out_shape=jax.ShapeDtypeStruct(features.shape, bf),
        in_specs=[hbm] * len(operands),
        out_specs=vmem,
        scratch_shapes=[
            *[pltpu.VMEM(a.shape, a.dtype) for a in operands],
            pltpu.VMEM((blocks, TAPS, TAPS, share), f32),
            pltpu.VMEM((rows + 2 * half, width, share), f32),
            pltpu.VMEM((rows, width, share), f32),
            pltpu.VMEM((rows, width, share), bf),
            pltpu.VMEM((blocks, 2, half, width, share), bf),
            pltpu.VMEM((blocks, rows, CORES, width, share), bf),
            pltpu.VMEM((blocks, rows, CORES, 1, width), f32),
            pltpu.VMEM((rows // 2 * width, depth), bf),
            pltpu.VMEM((rows // 2 * width, units), bf),
            pltpu.VMEM((blocks, rows, 2, width, share), bf),
            pltpu.VMEM((blocks, rows, 2, width, share), bf),
            pltpu.VMEM((blocks, rows, width, share), bf),
            pltpu.VMEM((blocks, rows, width, share), bf),
            pltpu.VMEM((rows, width, share), f32),
            dma((blocks, 2)),
            dma((7,)),
            dma((blocks, 2, half)),
            dma((blocks, 2, half)),
            dma((blocks, rows, 6)),
            dma((blocks, rows, 6)),
            dma((blocks, rows)),
            dma((blocks, rows)),
            dma((blocks, rows)),
            dma((blocks, rows)),
        ],
        compiler_params=pltpu.CompilerParams(
            collective_id=0, has_side_effects=True, vmem_limit_bytes=64 * 1024 * 1024
        ),
    )(*operands)


def solution(mesh):
    sizes = dict(mesh.shape)

    def body(features, *rest):
        if sizes["tensor"] == CORES and features.shape == (TAPS // 2 + 1, 128, 256):
            return fused(sizes["space"], features, *rest)
        return per_device(features, *rest)

    return jax.shard_map(
        body,
        mesh=mesh,
        in_specs=(
            P("space", None, "tensor"),
            P(None, None, None, "tensor"),
            P(),
            P(),
            P(None, None, "tensor"),
            P(None, "tensor"),
            P(None, "tensor", None),
            P(None, "tensor"),
            P(None, "tensor"),
        ),
        out_specs=P("space", None, "tensor"),
        check_vma=False,
    )
```

```python
import functools

import jax
import jax.numpy as jnp
from jax import lax
from jax.experimental import pallas as pl
from jax.experimental.pallas import tpu as pltpu
from jax.sharding import PartitionSpec as P

D = 1024
TAPS = 7
BLOCKS = 2


def with_halo(x, sides, width):
    for axis, dim in sides:
        devices, length = (lax.axis_size(axis), x.shape[dim])
        up = [(i, (i + 1) % devices) for i in range(devices - 1)]
        down = [(j, i) for i, j in up]
        last = lax.slice_in_dim(x, length - width, length, axis=dim)
        leading = lax.slice_in_dim(x, 0, width, axis=dim)
        before = lax.ppermute(last, axis, up)
        after = lax.ppermute(leading, axis, down)
        x = jnp.concatenate([before, x, after], axis=dim)
    return x


def one_block(stream, kernel, gain, bias, expand, bias_expand, reduce_w, bias_reduce, scale):
    half = TAPS // 2
    height, width, share = stream.shape
    positions = height * width
    padded = with_halo(stream, (("space", 0),), half)
    padded = jnp.pad(padded.astype(jnp.float32), ((0, 0), (half, half), (0, 0)))
    filtered = jnp.zeros(stream.shape, jnp.float32)
    for row_tap in range(TAPS):
        for col_tap in range(TAPS):
            filtered = filtered + padded[
                row_tap : row_tap + height, col_tap : col_tap + width
            ] * kernel[row_tap, col_tap].astype(jnp.float32)
    filtered = filtered.reshape(positions, share)
    offset = lax.axis_index("tensor") * share
    gain_part = lax.dynamic_slice_in_dim(gain, offset, share, 0)
    bias_part = lax.dynamic_slice_in_dim(bias, offset, share, 0)
    sums, squares = lax.psum(
        (jnp.sum(filtered, axis=-1), jnp.sum(filtered * filtered, axis=-1)), "tensor"
    )
    mean = (sums / D)[:, None]
    var = jnp.maximum(squares[:, None] / D - mean * mean, 0.0)
    normed_part = ((filtered - mean) / jnp.sqrt(var + 1e-06) * gain_part + bias_part).astype(
        jnp.bfloat16
    )
    preact = jnp.dot(
        lax.all_gather(normed_part, "tensor", axis=1, tiled=True),
        expand,
        preferred_element_type=jnp.float32,
    )
    hidden = jax.nn.gelu(preact + bias_expand, approximate=False).astype(jnp.bfloat16)
    partial_value = jnp.dot(hidden, reduce_w, preferred_element_type=jnp.float32)
    mixed = lax.psum_scatter(
        partial_value.astype(jnp.bfloat16), "tensor", scatter_dimension=1, tiled=True
    ).astype(jnp.float32)
    updated = stream.reshape(positions, share).astype(jnp.float32) + scale * (mixed + bias_reduce)
    return updated.astype(jnp.bfloat16).reshape(height, width, share)


def per_device(
    features,
    depth_kernel,
    norm_gain,
    norm_bias,
    w_expand,
    b_expand,
    w_reduce,
    b_reduce,
    layer_scale,
):
    stream = features
    for block_id in range(BLOCKS):
        stream = one_block(
            stream,
            depth_kernel[block_id],
            norm_gain[block_id],
            norm_bias[block_id],
            w_expand[block_id],
            b_expand[block_id],
            w_reduce[block_id],
            b_reduce[block_id],
            layer_scale[block_id],
        )
    return stream


MESH = pl.DeviceIdType.MESH
CORES = 4


def shift_down(x, first):
    return jnp.where(first, 0.0, pltpu.roll(x, 1, 0))


def shift_up(x, last):
    return jnp.where(last, 0.0, pltpu.roll(x, x.shape[0] - 1, 0))


def blocks_kernel(
    n_space, feat_in, taps_in, gain_in, nbias_in, w1_in, b1_in, w2_in, b2_in, scale_in, out,
    feat, taps, gain, nbias, w1, b1, w2, b2, scale, taps32, xf, filt, mid, halo, gathered, centers, normed, hidden,
    parts, pair_in, cross_in, deltas,
    w_sem, in_sem, halo_send, halo_recv, ag_send, ag_recv, pair_send, pair_recv, cross_send, cross_recv,
):
    rows, width, share = feat.shape
    half = TAPS // 2
    blocks = w1.shape[0]
    band = lax.axis_index("space")
    me = lax.axis_index("tensor")
    core = lax.rem(me, 2)
    mate = me + 1 - 2 * core
    across = lax.rem(me + 2, CORES)
    diagonal = lax.rem(mate + 2, CORES)
    has_up = band > 0
    has_down = band < n_space - 1

    def weight_copies(b):
        return (
            pltpu.make_async_copy(w1_in.at[b], w1.at[b], w_sem.at[b, 0]),
            pltpu.make_async_copy(w2_in.at[b], w2.at[b], w_sem.at[b, 1]),
        )

    pairs_in = (
        (feat_in, feat), (taps_in, taps), (gain_in, gain), (nbias_in, nbias),
        (b1_in, b1), (b2_in, b2), (scale_in, scale),
    )
    small_copies = [
        pltpu.make_async_copy(src, dst, in_sem.at[i]) for i, (src, dst) in enumerate(pairs_in)
    ]
    for copy in small_copies:
        copy.start()
    for b in range(blocks):
        for copy in weight_copies(b):
            copy.start()

    barrier = pltpu.get_barrier_semaphore()
    for who in (mate, across):
        pl.semaphore_signal(barrier, inc=1, device_id=(band, who), device_id_type=MESH)

    @pl.when(has_up)
    def _():
        pl.semaphore_signal(barrier, inc=1, device_id=(band - 1, me), device_id_type=MESH)

    @pl.when(has_down)
    def _():
        pl.semaphore_signal(barrier, inc=1, device_id=(band + 1, me), device_id_type=MESH)

    pl.semaphore_wait(barrier, 2 + jnp.minimum(band, 1) + jnp.minimum(n_space - 1 - band, 1))

    def remote(src, dst, send, recv, who):
        return pltpu.make_async_remote_copy(
            src_ref=src, dst_ref=dst, send_sem=send, recv_sem=recv, device_id=who, device_id_type=MESH
        )

    def halo_copy(b, source, side, i):
        row = i if side == 0 else rows - half + i
        target = (band - 1, me) if side == 0 else (band + 1, me)
        return remote(
            source.at[row], halo.at[b, side, i], halo_send.at[b, side, i], halo_recv.at[b, side, i], target
        )

    present = (has_up, has_down)

    def ag_copy(b, r, kind):
        slot, target = ((me, mate), (me, across), (across, mate))[kind % 3]
        ref = (gathered if kind < 3 else centers).at[b, r, slot]
        return remote(ref, ref, ag_send.at[b, r, kind], ag_recv.at[b, r, kind], (band, target))

    def pair_copy(b, r):
        return remote(
            parts.at[b, r, pl.ds(0, 2)], pair_in.at[b, r], pair_send.at[b, r], pair_recv.at[b, r], (band, mate)
        )

    def cross_copy(b, r):
        return remote(
            parts.at[b, r, 3], cross_in.at[b, r], cross_send.at[b, r], cross_recv.at[b, r], (band, across)
        )

    column = lax.broadcasted_iota(jnp.int32, (width, 128), 0)
    lane = lax.broadcasted_iota(jnp.int32, (width, 128), 1)
    first, last, diag = column == 0, column == width - 1, column == lane

    def convolve(b, r, pairs):
        def part(h, fresh):
            ch = pl.ds(pl.multiple_of(h * 128, 128), 128)

            def along(j):
                total = None
                for row, tap in pairs:
                    term = xf[row, :, ch] * taps32[b, tap, pl.ds(j, 1), ch]
                    total = term if total is None else total + term
                return total

            right = shift_down(along(0), first)
            for j in range(1, half):
                right = shift_down(right + along(j), first)
            left = shift_up(along(TAPS - 1), last)
            for j in range(TAPS - 2, half, -1):
                left = shift_up(left + along(j), last)
            total = along(half) + right + left
            if not fresh:
                total = total + filt[r, :, ch]
            filt[r, :, ch] = total

        return part

    def early_rows(b):
        if b == 0:
            return range(rows)
        return range(rows - 1) if b % 2 == 1 else range(1, rows)

    def conv_own(b):
        def body(step, carry):
            r, h = step // (share // 128), lax.rem(step, share // 128)
            convolve(b, r, [(half + m, half + m - r) for m in early_rows(b)])(h, True)
            return carry

        lax.fori_loop(0, rows * (share // 128), body, 0)

    def conv_halo(b, r):
        pairs = [(half + m, half + m - r) for m in range(rows) if m not in early_rows(b)]
        for m in range(half):
            row = r + m + rows * ((r + m) // half)
            pairs.append((row, row - r))

        def body(h, carry):
            convolve(b, r, pairs)(h, False)
            return carry

        lax.fori_loop(0, share // 128, body, 0)

    def take_halo(b, upper, i):
        side, base, there = (1, 0, has_up) if upper else (0, half + rows, has_down)

        @pl.when(there)
        def _():
            halo_copy(b, mid, side, i).wait_recv()
            xf[base + i] = halo[b, side, i].astype(jnp.float32)

        @pl.when(jnp.logical_not(there))
        def _():
            xf[base + i] = jnp.zeros((width, share), jnp.float32)

    def send_filtered(b, r):
        value = filt[r]
        center = jnp.sum(value, axis=1, keepdims=True) / share
        gathered[b, r, me] = (value - center).astype(jnp.bfloat16)
        centers[b, r, me] = jnp.sum(jnp.where(diag, center, 0.0), axis=0, keepdims=True)
        for kind in (4, 1, 3, 0):
            ag_copy(b, r, kind).start()

    def normalize(b, r):
        def own_mean(s, total):
            mean = jnp.sum(jnp.where(diag, centers[b, r, s], 0.0), axis=1, keepdims=True)
            deltas[s] = mean
            return total + mean

        mean = lax.fori_loop(0, CORES, own_mean, jnp.zeros((width, 1), jnp.float32)) / CORES

        def square(s, total):
            value = gathered[b, r, s].astype(jnp.float32) + (deltas[s] - mean)
            return total + value * value

        squares = lax.fori_loop(0, CORES, square, jnp.zeros((width, share), jnp.float32))
        inverse = lax.rsqrt(jnp.sum(squares, axis=1, keepdims=True) / (share * CORES) + 1e-06)

        def write(s, carry):
            ch = pl.ds(pl.multiple_of(s * share, share), share)
            value = gathered[b, r, s].astype(jnp.float32) + (deltas[s] - mean)
            value = value * inverse * gain[pl.ds(b, 1), ch] + nbias[pl.ds(b, 1), ch]
            normed[:, ch] = value.astype(jnp.bfloat16)
            return carry

        lax.fori_loop(0, CORES, write, 0)

    def expand(b):
        def tile(n, carry):
            ch = pl.ds(pl.multiple_of(n * 256, 256), 256)
            x = jnp.dot(normed[...], w1[b, :, ch], preferred_element_type=jnp.float32) + b1[pl.ds(b, 1), ch]
            hidden[:, ch] = (0.5 * x * (1.0 + lax.erf(x * 0.7071067811865476))).astype(jnp.bfloat16)
            return carry

        lax.fori_loop(0, w1.shape[2] // 256, tile, 0)

    def reduce_all(b, r):
        def tile(j, carry):
            owner = lax.rem(mate + (j // 2) * (me - mate) + 2 * lax.rem(j, 2), CORES)
            ch = pl.ds(pl.multiple_of(owner * share, share), share)
            value = jnp.dot(hidden[...], w2[b, :, ch], preferred_element_type=jnp.float32)
            parts[b, r, j] = value.astype(jnp.bfloat16)

            @pl.when(j == 1)
            def _():
                pair_copy(b, r).start()

            return carry

        lax.fori_loop(0, CORES, tile, 0)

    def pair_sum(b, r):
        pair_copy(b, r).wait_recv()
        total = parts[b, r, 3].astype(jnp.float32) + pair_in[b, r, 1].astype(jnp.float32)
        parts[b, r, 3] = total.astype(jnp.bfloat16)
        cross_copy(b, r).start()

    def finish(b, r):
        cross_copy(b, r).wait_recv()
        mixed = parts[b, r, 2].astype(jnp.float32) + pair_in[b, r, 0].astype(jnp.float32) + cross_in[b, r].astype(jnp.float32)
        before = (feat if b == 0 else mid)[r].astype(jnp.float32)
        new = (before + scale[pl.ds(b, 1), :] * (mixed + b2[pl.ds(b, 1), :])).astype(jnp.bfloat16)
        if b == blocks - 1:
            out[r] = new
            return
        mid[r] = new
        xf[half + r] = new.astype(jnp.float32)

    def send_halo(b, source, side, i):
        @pl.when(present[side])
        def _():
            halo_copy(b, source, side, i).start()

    for i in range(half):
        send_halo(0, feat_in, 1, i)
    for copy in small_copies:
        copy.wait()
    for b in range(blocks):
        taps32[b] = taps[:, :, b, :].astype(jnp.float32)
    for r in range(rows):
        xf[half + r] = feat[r].astype(jnp.float32)

    for b in range(blocks):
        downward = b % 2 == 0
        row_of = (lambda k: k) if downward else (lambda k: rows - 1 - k)
        if b == 0:
            conv_own(b)

            @pl.when(has_down)
            def _():
                for i in range(half):
                    halo_copy(0, feat_in, 1, i).wait_send()

            for i in range(half):
                send_halo(0, feat_in, 0, i)
        else:
            send_halo(b, mid, 1 if not downward else 0, half - 2 if not downward else 1)

        for i in range(half):
            take_halo(b, downward, i)

        def front(k, carry, b=b, row_of=row_of, downward=downward):
            r = row_of(k)

            @pl.when(k > 0)
            def _():
                take_halo(b, not downward, k - 1 if downward else rows - 1 - k)

            conv_halo(b, r)
            send_filtered(b, r)
            return carry

        if b > 0:
            front(0, 0)
            send_halo(b, mid, 1 if not downward else 0, 0 if not downward else half - 1)
            lax.fori_loop(1, rows, front, 0)
        else:
            lax.fori_loop(0, rows, front, 0)
        for copy in weight_copies(b):
            copy.wait()

        def relay(r, b=b):
            for kind in (4, 1):
                ag_copy(b, r, kind).wait_recv()
                ag_copy(b, r, kind + 1).start()

        def arrive(r, b=b):
            for kind in (0, 3, 2, 5):
                ag_copy(b, r, kind).wait_recv()

        def finish_and_send(k, b=b, row_of=row_of, downward=downward):
            r = row_of(k)
            finish(b, r)
            if b < blocks - 1:
                send_halo(b + 1, mid, 0 if downward else 1, r if downward else r - (rows - half))

        relay(row_of(0))

        def middle(k, carry, b=b, row_of=row_of):
            r = row_of(k)
            arrive(r)
            normalize(b, r)
            expand(b)

            @pl.when(k < rows - 1)
            def _():
                relay(row_of(k + 1))

            @pl.when(k > 0)
            def _():
                pair_sum(b, row_of(k - 1))

            reduce_all(b, r)

            @pl.when(k > 1)
            def _():
                finish_and_send(k - 2)

            return carry

        lax.fori_loop(0, rows, middle, 0)
        pair_sum(b, row_of(rows - 1))
        finish_and_send(rows - 2)
        if b < blocks - 1:
            conv_own(b + 1)
        finish(b, row_of(rows - 1))
        if b < blocks - 1:
            send_halo(b + 1, mid, 1 if downward else 0, half - 1 if downward else 0)

    for b in range(blocks):
        for side in range(2):
            if b == 0 and side == 1:
                continue

            @pl.when(present[side])
            def _(b=b, side=side):
                for i in range(half):
                    halo_copy(b, feat_in if b == 0 else mid, side, i).wait_send()

        def drain(r, carry, b=b):
            for kind in range(6):
                ag_copy(b, r, kind).wait_send()
            pair_copy(b, r).wait_send()
            cross_copy(b, r).wait_send()
            return carry

        lax.fori_loop(0, rows, drain, 0)


def fused(n_space, features, depth_kernel, gain, nbias, w1, b1, w2, b2, scale):
    rows, width, share = features.shape
    blocks, depth, units = w1.shape
    half = TAPS // 2
    depth_kernel = jnp.transpose(depth_kernel, (1, 2, 0, 3))
    operands = (features, depth_kernel, gain, nbias, w1, b1, w2, b2, scale)
    vmem = pl.BlockSpec(memory_space=pltpu.VMEM)
    hbm = pl.BlockSpec(memory_space=pl.ANY)
    bf, f32 = jnp.bfloat16, jnp.float32
    dma = pltpu.SemaphoreType.DMA
    return pl.pallas_call(
        functools.partial(blocks_kernel, n_space),
        out_shape=jax.ShapeDtypeStruct(features.shape, bf),
        in_specs=[hbm] * len(operands),
        out_specs=vmem,
        scratch_shapes=[
            *[pltpu.VMEM(a.shape, a.dtype) for a in operands],
            pltpu.VMEM((blocks, TAPS, TAPS, share), f32),
            pltpu.VMEM((rows + 2 * half, width, share), f32),
            pltpu.VMEM((rows, width, share), f32),
            pltpu.VMEM((rows, width, share), bf),
            pltpu.VMEM((blocks, 2, half, width, share), bf),
            pltpu.VMEM((blocks, rows, CORES, width, share), bf),
            pltpu.VMEM((blocks, rows, CORES, 1, width), f32),
            pltpu.VMEM((width, depth), bf),
            pltpu.VMEM((width, units), bf),
            pltpu.VMEM((blocks, rows, CORES, width, share), bf),
            pltpu.VMEM((blocks, rows, 2, width, share), bf),
            pltpu.VMEM((blocks, rows, width, share), bf),
            pltpu.VMEM((CORES, width, 1), f32),
            dma((blocks, 2)),
            dma((7,)),
            dma((blocks, 2, half)),
            dma((blocks, 2, half)),
            dma((blocks, rows, 6)),
            dma((blocks, rows, 6)),
            dma((blocks, rows)),
            dma((blocks, rows)),
            dma((blocks, rows)),
            dma((blocks, rows)),
        ],
        compiler_params=pltpu.CompilerParams(
            collective_id=0, has_side_effects=True, vmem_limit_bytes=64 * 1024 * 1024
        ),
    )(*operands)


def solution(mesh):
    sizes = dict(mesh.shape)

    def body(features, *rest):
        if sizes["tensor"] == CORES and features.shape == (TAPS // 2 + 1, 128, 256):
            return fused(sizes["space"], features, *rest)
        return per_device(features, *rest)

    return jax.shard_map(
        body,
        mesh=mesh,
        in_specs=(
            P("space", None, "tensor"),
            P(None, None, None, "tensor"),
            P(),
            P(),
            P(None, None, "tensor"),
            P(None, "tensor"),
            P(None, "tensor", None),
            P(None, "tensor"),
            P(None, "tensor"),
        ),
        out_specs=P("space", None, "tensor"),
        check_vma=False,
    )
```

```python
import functools

import jax
import jax.numpy as jnp
from jax import lax
from jax.experimental import pallas as pl
from jax.experimental.pallas import tpu as pltpu
from jax.sharding import PartitionSpec as P

D = 1024
TAPS = 7
BLOCKS = 2


def with_halo(x, sides, width):
    for axis, dim in sides:
        devices, length = (lax.axis_size(axis), x.shape[dim])
        up = [(i, (i + 1) % devices) for i in range(devices - 1)]
        down = [(j, i) for i, j in up]
        last = lax.slice_in_dim(x, length - width, length, axis=dim)
        leading = lax.slice_in_dim(x, 0, width, axis=dim)
        before = lax.ppermute(last, axis, up)
        after = lax.ppermute(leading, axis, down)
        x = jnp.concatenate([before, x, after], axis=dim)
    return x


def one_block(stream, kernel, gain, bias, expand, bias_expand, reduce_w, bias_reduce, scale):
    half = TAPS // 2
    height, width, share = stream.shape
    positions = height * width
    padded = with_halo(stream, (("space", 0),), half)
    padded = jnp.pad(padded.astype(jnp.float32), ((0, 0), (half, half), (0, 0)))
    filtered = jnp.zeros(stream.shape, jnp.float32)
    for row_tap in range(TAPS):
        for col_tap in range(TAPS):
            filtered = filtered + padded[
                row_tap : row_tap + height, col_tap : col_tap + width
            ] * kernel[row_tap, col_tap].astype(jnp.float32)
    filtered = filtered.reshape(positions, share)
    offset = lax.axis_index("tensor") * share
    gain_part = lax.dynamic_slice_in_dim(gain, offset, share, 0)
    bias_part = lax.dynamic_slice_in_dim(bias, offset, share, 0)
    sums, squares = lax.psum(
        (jnp.sum(filtered, axis=-1), jnp.sum(filtered * filtered, axis=-1)), "tensor"
    )
    mean = (sums / D)[:, None]
    var = jnp.maximum(squares[:, None] / D - mean * mean, 0.0)
    normed_part = ((filtered - mean) / jnp.sqrt(var + 1e-06) * gain_part + bias_part).astype(
        jnp.bfloat16
    )
    preact = jnp.dot(
        lax.all_gather(normed_part, "tensor", axis=1, tiled=True),
        expand,
        preferred_element_type=jnp.float32,
    )
    hidden = jax.nn.gelu(preact + bias_expand, approximate=False).astype(jnp.bfloat16)
    partial_value = jnp.dot(hidden, reduce_w, preferred_element_type=jnp.float32)
    mixed = lax.psum_scatter(
        partial_value.astype(jnp.bfloat16), "tensor", scatter_dimension=1, tiled=True
    ).astype(jnp.float32)
    updated = stream.reshape(positions, share).astype(jnp.float32) + scale * (mixed + bias_reduce)
    return updated.astype(jnp.bfloat16).reshape(height, width, share)


def per_device(
    features,
    depth_kernel,
    norm_gain,
    norm_bias,
    w_expand,
    b_expand,
    w_reduce,
    b_reduce,
    layer_scale,
):
    stream = features
    for block_id in range(BLOCKS):
        stream = one_block(
            stream,
            depth_kernel[block_id],
            norm_gain[block_id],
            norm_bias[block_id],
            w_expand[block_id],
            b_expand[block_id],
            w_reduce[block_id],
            b_reduce[block_id],
            layer_scale[block_id],
        )
    return stream


MESH = pl.DeviceIdType.MESH
CORES = 4


def shift_down(x, first):
    return jnp.where(first, 0.0, pltpu.roll(x, 1, 0))


def shift_up(x, last):
    return jnp.where(last, 0.0, pltpu.roll(x, x.shape[0] - 1, 0))


def blocks_kernel(
    n_space, feat_in, taps_in, gain_in, nbias_in, w1_in, b1_in, w2_in, b2_in, scale_in, out,
    feat, taps, gain, nbias, w1, b1, w2, b2, scale, taps32, xf, filt, mid, last_rows, halo, gathered, centers, normed, hidden,
    pair_out, pair_in, cross_out, cross_in, own,
    w_sem, in_sem, out_sem, halo_send, halo_recv, ag_send, ag_recv, pair_send, pair_recv, cross_send, cross_recv,
):
    rows, width, share = feat.shape
    half = TAPS // 2
    blocks = w1.shape[0]
    band = lax.axis_index("space")
    me = lax.axis_index("tensor")
    core = lax.rem(me, 2)
    mate = me + 1 - 2 * core
    across = lax.rem(me + 2, CORES)
    diagonal = lax.rem(mate + 2, CORES)
    has_up = band > 0
    has_down = band < n_space - 1

    def weight_copies(b):
        return (
            pltpu.make_async_copy(w1_in.at[b], w1.at[b], w_sem.at[b, 0]),
            pltpu.make_async_copy(w2_in.at[b], w2.at[b], w_sem.at[b, 1]),
        )

    pairs_in = (
        (feat_in, feat), (taps_in, taps), (gain_in, gain), (nbias_in, nbias),
        (b1_in, b1), (b2_in, b2), (scale_in, scale),
    )
    small_copies = [
        pltpu.make_async_copy(src, dst, in_sem.at[i]) for i, (src, dst) in enumerate(pairs_in)
    ]
    for copy in small_copies:
        copy.start()
    for b in range(blocks):
        for copy in weight_copies(b):
            copy.start()

    barrier = pltpu.get_barrier_semaphore()
    for who in (mate, across):
        pl.semaphore_signal(barrier, inc=1, device_id=(band, who), device_id_type=MESH)

    @pl.when(has_up)
    def _():
        pl.semaphore_signal(barrier, inc=1, device_id=(band - 1, me), device_id_type=MESH)

    @pl.when(has_down)
    def _():
        pl.semaphore_signal(barrier, inc=1, device_id=(band + 1, me), device_id_type=MESH)

    pl.semaphore_wait(barrier, 2 + jnp.minimum(band, 1) + jnp.minimum(n_space - 1 - band, 1))

    def remote(src, dst, send, recv, who):
        return pltpu.make_async_remote_copy(
            src_ref=src, dst_ref=dst, send_sem=send, recv_sem=recv, device_id=who, device_id_type=MESH
        )

    def halo_copy(b, source, side, i):
        row = i if side == 0 else rows - half + i
        target = (band - 1, me) if side == 0 else (band + 1, me)
        return remote(
            source.at[row], halo.at[b, side, i], halo_send.at[b, side, i], halo_recv.at[b, side, i], target
        )

    present = (has_up, has_down)

    def ag_copy(b, r, kind):
        slot, target = ((me, mate), (me, across), (across, mate))[kind % 3]
        ref = (gathered if kind < 3 else centers).at[b, r, slot]
        return remote(ref, ref, ag_send.at[b, r, kind], ag_recv.at[b, r, kind], (band, target))

    def pair_copy(b, r):
        return remote(
            pair_out.at[b, r], pair_in.at[b, r], pair_send.at[b, r], pair_recv.at[b, r], (band, mate)
        )

    def cross_copy(b, r):
        return remote(
            cross_out.at[b, r], cross_in.at[b, r], cross_send.at[b, r], cross_recv.at[b, r], (band, across)
        )

    column = lax.broadcasted_iota(jnp.int32, (width, 128), 0)
    lane = lax.broadcasted_iota(jnp.int32, (width, 128), 1)
    first, last, diag = column == 0, column == width - 1, column == lane

    def convolve(b, r, pairs):
        def part(h, fresh):
            ch = pl.ds(pl.multiple_of(h * 128, 128), 128)

            def along(j):
                total = None
                for row, tap in pairs:
                    term = xf[row, :, ch] * taps32[b, tap, pl.ds(j, 1), ch]
                    total = term if total is None else total + term
                return total

            right = shift_down(along(0), first)
            for j in range(1, half):
                right = shift_down(right + along(j), first)
            left = shift_up(along(TAPS - 1), last)
            for j in range(TAPS - 2, half, -1):
                left = shift_up(left + along(j), last)
            total = along(half) + right + left
            if not fresh:
                total = total + filt[r, :, ch]
            filt[r, :, ch] = total

        return part

    def early_rows(b):
        if b == 0:
            return range(rows)
        return range(rows - 1) if b % 2 == 1 else range(1, rows)

    def conv_own(b):
        def body(step, carry):
            r, h = step // (share // 128), lax.rem(step, share // 128)
            convolve(b, r, [(half + m, half + m - r) for m in early_rows(b)])(h, True)
            return carry

        lax.fori_loop(0, rows * (share // 128), body, 0)

    def conv_halo(b, r):
        pairs = [(half + m, half + m - r) for m in range(rows) if m not in early_rows(b)]
        for m in range(half):
            row = r + m + rows * ((r + m) // half)
            pairs.append((row, row - r))

        def body(h, carry):
            convolve(b, r, pairs)(h, False)
            return carry

        lax.fori_loop(0, share // 128, body, 0)

    def take_halo(b, upper, i):
        side, base, there = (1, 0, has_up) if upper else (0, half + rows, has_down)

        @pl.when(there)
        def _():
            halo_copy(b, mid, side, i).wait_recv()
            xf[base + i] = halo[b, side, i].astype(jnp.float32)

        @pl.when(jnp.logical_not(there))
        def _():
            xf[base + i] = jnp.zeros((width, share), jnp.float32)

    def send_filtered(b, r):
        value = filt[r]
        center = jnp.sum(value, axis=1, keepdims=True) / share
        gathered[b, r, me] = (value - center).astype(jnp.bfloat16)
        centers[b, r, me] = jnp.sum(jnp.where(diag, center, 0.0), axis=0, keepdims=True)
        for kind in (4, 1, 3, 0):
            ag_copy(b, r, kind).start()

    def normalize(b, r):
        own_means = [
            jnp.sum(jnp.where(diag, centers[b, r, s], 0.0), axis=1, keepdims=True) for s in range(CORES)
        ]
        mean = (own_means[0] + own_means[1] + own_means[2] + own_means[3]) / CORES
        deltas = [c - mean for c in own_means]
        squares = jnp.zeros((width, share), jnp.float32)
        for s in range(CORES):
            value = gathered[b, r, s].astype(jnp.float32) + deltas[s]
            squares = squares + value * value
        var = jnp.sum(squares, axis=1, keepdims=True) / (share * CORES)
        inverse = lax.rsqrt(var + 1e-06)
        for s in range(CORES):
            ch = pl.ds(s * share, share)
            value = gathered[b, r, s].astype(jnp.float32) + deltas[s]
            value = value * inverse * gain[pl.ds(b, 1), ch] + nbias[pl.ds(b, 1), ch]
            normed[:, ch] = value.astype(jnp.bfloat16)

    def expand(b):
        for n in range(w1.shape[2] // 256):
            ch = pl.ds(n * 256, 256)
            x = jnp.dot(normed[...], w1[b, :, ch], preferred_element_type=jnp.float32) + b1[pl.ds(b, 1), ch]
            hidden[:, ch] = (0.5 * x * (1.0 + lax.erf(x * 0.7071067811865476))).astype(jnp.bfloat16)

    def reduce_to(b, owner):
        ch = pl.ds(pl.multiple_of(owner * share, share), share)
        return jnp.dot(hidden[...], w2[b, :, ch], preferred_element_type=jnp.float32)

    def pair_sum(b, r):
        pair_copy(b, r).wait_recv()
        total = cross_out[b, r].astype(jnp.float32) + pair_in[b, r, 1].astype(jnp.float32)
        cross_out[b, r] = total.astype(jnp.bfloat16)
        cross_copy(b, r).start()

    def out_copy(r):
        return pltpu.make_async_copy(last_rows.at[r], out.at[r], out_sem.at[r])

    def finish(b, r):
        cross_copy(b, r).wait_recv()
        mixed = own[r] + pair_in[b, r, 0].astype(jnp.float32) + cross_in[b, r].astype(jnp.float32)
        before = (feat if b == 0 else mid)[r].astype(jnp.float32)
        new = (before + scale[pl.ds(b, 1), :] * (mixed + b2[pl.ds(b, 1), :])).astype(jnp.bfloat16)
        if b == blocks - 1:
            last_rows[r] = new
            out_copy(r).start()
            return
        mid[r] = new
        xf[half + r] = new.astype(jnp.float32)

    def send_halo(b, source, side, i):
        @pl.when(present[side])
        def _():
            halo_copy(b, source, side, i).start()

    for i in range(half):
        send_halo(0, feat_in, 1, i)
    for copy in small_copies:
        copy.wait()
    for b in range(blocks):
        taps32[b] = taps[:, :, b, :].astype(jnp.float32)
    for r in range(rows):
        xf[half + r] = feat[r].astype(jnp.float32)

    for b in range(blocks):
        downward = b % 2 == 0
        row_of = (lambda k: k) if downward else (lambda k: rows - 1 - k)
        if b == 0:
            conv_own(b)

            @pl.when(has_down)
            def _():
                for i in range(half):
                    halo_copy(0, feat_in, 1, i).wait_send()

            for i in range(half):
                send_halo(0, feat_in, 0, i)
        else:
            send_halo(b, mid, 1 if not downward else 0, half - 2 if not downward else 1)

        for i in range(half):
            take_halo(b, downward, i)

        def front(k, carry, b=b, row_of=row_of, downward=downward):
            r = row_of(k)

            @pl.when(k > 0)
            def _():
                take_halo(b, not downward, k - 1 if downward else rows - 1 - k)

            conv_halo(b, r)
            send_filtered(b, r)
            return carry

        if b > 0:
            front(0, 0)
            send_halo(b, mid, 1 if not downward else 0, 0 if not downward else half - 1)
            lax.fori_loop(1, rows, front, 0)
        else:
            lax.fori_loop(0, rows, front, 0)
        for copy in weight_copies(b):
            copy.wait()

        def relay(r, b=b):
            for kind in (4, 1):
                ag_copy(b, r, kind).wait_recv()
                ag_copy(b, r, kind + 1).start()

        def arrive(r, b=b):
            for kind in (0, 3, 2, 5):
                ag_copy(b, r, kind).wait_recv()

        def send_partials(r, b=b):
            pair_out[b, r, 0] = reduce_to(b, mate).astype(jnp.bfloat16)
            pair_out[b, r, 1] = reduce_to(b, diagonal).astype(jnp.bfloat16)
            pair_copy(b, r).start()

        def keep_partials(r, b=b):
            own[r] = reduce_to(b, me)
            cross_out[b, r] = reduce_to(b, across).astype(jnp.bfloat16)

        def finish_and_send(k, b=b, row_of=row_of, downward=downward):
            r = row_of(k)
            finish(b, r)
            if b < blocks - 1:
                send_halo(b + 1, mid, 0 if downward else 1, r if downward else r - (rows - half))

        relay(row_of(0))

        def middle(k, carry, b=b, row_of=row_of):
            r = row_of(k)
            arrive(r)
            normalize(b, r)
            expand(b)

            @pl.when(k < rows - 1)
            def _():
                relay(row_of(k + 1))

            @pl.when(k > 0)
            def _():
                pair_sum(b, row_of(k - 1))

            send_partials(r)
            keep_partials(r)

            @pl.when(k > 1)
            def _():
                finish_and_send(k - 2)

            return carry

        lax.fori_loop(0, rows, middle, 0)
        pair_sum(b, row_of(rows - 1))
        finish_and_send(rows - 2)
        if b < blocks - 1:
            conv_own(b + 1)
        finish(b, row_of(rows - 1))
        if b < blocks - 1:
            send_halo(b + 1, mid, 1 if downward else 0, half - 1 if downward else 0)

    for r in range(rows):
        out_copy(r).wait()
    for b in range(blocks):
        for side in range(2):
            if b == 0 and side == 1:
                continue

            @pl.when(present[side])
            def _(b=b, side=side):
                for i in range(half):
                    halo_copy(b, feat_in if b == 0 else mid, side, i).wait_send()

        def drain(r, carry, b=b):
            for kind in range(6):
                ag_copy(b, r, kind).wait_send()
            pair_copy(b, r).wait_send()
            cross_copy(b, r).wait_send()
            return carry

        lax.fori_loop(0, rows, drain, 0)


def fused(n_space, features, depth_kernel, gain, nbias, w1, b1, w2, b2, scale):
    rows, width, share = features.shape
    blocks, depth, units = w1.shape
    half = TAPS // 2
    depth_kernel = jnp.transpose(depth_kernel, (1, 2, 0, 3))
    operands = (features, depth_kernel, gain, nbias, w1, b1, w2, b2, scale)
    hbm = pl.BlockSpec(memory_space=pl.ANY)
    bf, f32 = jnp.bfloat16, jnp.float32
    dma = pltpu.SemaphoreType.DMA
    return pl.pallas_call(
        functools.partial(blocks_kernel, n_space),
        out_shape=jax.ShapeDtypeStruct(features.shape, bf),
        in_specs=[hbm] * len(operands),
        out_specs=hbm,
        scratch_shapes=[
            *[pltpu.VMEM(a.shape, a.dtype) for a in operands],
            pltpu.VMEM((blocks, TAPS, TAPS, share), f32),
            pltpu.VMEM((rows + 2 * half, width, share), f32),
            pltpu.VMEM((rows, width, share), f32),
            pltpu.VMEM((rows, width, share), bf),
            pltpu.VMEM((rows, width, share), bf),
            pltpu.VMEM((blocks, 2, half, width, share), bf),
            pltpu.VMEM((blocks, rows, CORES, width, share), bf),
            pltpu.VMEM((blocks, rows, CORES, 1, width), f32),
            pltpu.VMEM((width, depth), bf),
            pltpu.VMEM((width, units), bf),
            pltpu.VMEM((blocks, rows, 2, width, share), bf),
            pltpu.VMEM((blocks, rows, 2, width, share), bf),
            pltpu.VMEM((blocks, rows, width, share), bf),
            pltpu.VMEM((blocks, rows, width, share), bf),
            pltpu.VMEM((rows, width, share), f32),
            dma((blocks, 2)),
            dma((7,)),
            dma((rows,)),
            dma((blocks, 2, half)),
            dma((blocks, 2, half)),
            dma((blocks, rows, 6)),
            dma((blocks, rows, 6)),
            dma((blocks, rows)),
            dma((blocks, rows)),
            dma((blocks, rows)),
            dma((blocks, rows)),
        ],
        compiler_params=pltpu.CompilerParams(
            collective_id=0, has_side_effects=True, vmem_limit_bytes=64 * 1024 * 1024
        ),
    )(*operands)


def solution(mesh):
    sizes = dict(mesh.shape)

    def body(features, *rest):
        if sizes["tensor"] == CORES and features.shape == (TAPS // 2 + 1, 128, 256):
            return fused(sizes["space"], features, *rest)
        return per_device(features, *rest)

    return jax.shard_map(
        body,
        mesh=mesh,
        in_specs=(
            P("space", None, "tensor"),
            P(None, None, None, "tensor"),
            P(),
            P(),
            P(None, None, "tensor"),
            P(None, "tensor"),
            P(None, "tensor", None),
            P(None, "tensor"),
            P(None, "tensor"),
        ),
        out_specs=P("space", None, "tensor"),
        check_vma=False,
    )
```

```python
import functools

import jax
import jax.numpy as jnp
from jax import lax
from jax.experimental import pallas as pl
from jax.experimental.pallas import tpu as pltpu
from jax.sharding import PartitionSpec as P

D = 1024
TAPS = 7
BLOCKS = 2


def with_halo(x, sides, width):
    for axis, dim in sides:
        devices, length = (lax.axis_size(axis), x.shape[dim])
        up = [(i, (i + 1) % devices) for i in range(devices - 1)]
        down = [(j, i) for i, j in up]
        last = lax.slice_in_dim(x, length - width, length, axis=dim)
        leading = lax.slice_in_dim(x, 0, width, axis=dim)
        before = lax.ppermute(last, axis, up)
        after = lax.ppermute(leading, axis, down)
        x = jnp.concatenate([before, x, after], axis=dim)
    return x


def one_block(stream, kernel, gain, bias, expand, bias_expand, reduce_w, bias_reduce, scale):
    half = TAPS // 2
    height, width, share = stream.shape
    positions = height * width
    padded = with_halo(stream, (("space", 0),), half)
    padded = jnp.pad(padded.astype(jnp.float32), ((0, 0), (half, half), (0, 0)))
    filtered = jnp.zeros(stream.shape, jnp.float32)
    for row_tap in range(TAPS):
        for col_tap in range(TAPS):
            filtered = filtered + padded[
                row_tap : row_tap + height, col_tap : col_tap + width
            ] * kernel[row_tap, col_tap].astype(jnp.float32)
    filtered = filtered.reshape(positions, share)
    offset = lax.axis_index("tensor") * share
    gain_part = lax.dynamic_slice_in_dim(gain, offset, share, 0)
    bias_part = lax.dynamic_slice_in_dim(bias, offset, share, 0)
    sums, squares = lax.psum(
        (jnp.sum(filtered, axis=-1), jnp.sum(filtered * filtered, axis=-1)), "tensor"
    )
    mean = (sums / D)[:, None]
    var = jnp.maximum(squares[:, None] / D - mean * mean, 0.0)
    normed_part = ((filtered - mean) / jnp.sqrt(var + 1e-06) * gain_part + bias_part).astype(
        jnp.bfloat16
    )
    preact = jnp.dot(
        lax.all_gather(normed_part, "tensor", axis=1, tiled=True),
        expand,
        preferred_element_type=jnp.float32,
    )
    hidden = jax.nn.gelu(preact + bias_expand, approximate=False).astype(jnp.bfloat16)
    partial_value = jnp.dot(hidden, reduce_w, preferred_element_type=jnp.float32)
    mixed = lax.psum_scatter(
        partial_value.astype(jnp.bfloat16), "tensor", scatter_dimension=1, tiled=True
    ).astype(jnp.float32)
    updated = stream.reshape(positions, share).astype(jnp.float32) + scale * (mixed + bias_reduce)
    return updated.astype(jnp.bfloat16).reshape(height, width, share)


def per_device(
    features,
    depth_kernel,
    norm_gain,
    norm_bias,
    w_expand,
    b_expand,
    w_reduce,
    b_reduce,
    layer_scale,
):
    stream = features
    for block_id in range(BLOCKS):
        stream = one_block(
            stream,
            depth_kernel[block_id],
            norm_gain[block_id],
            norm_bias[block_id],
            w_expand[block_id],
            b_expand[block_id],
            w_reduce[block_id],
            b_reduce[block_id],
            layer_scale[block_id],
        )
    return stream


MESH = pl.DeviceIdType.MESH
CORES = 4


def shift_down(x, first):
    return jnp.where(first, 0.0, pltpu.roll(x, 1, 0))


def shift_up(x, last):
    return jnp.where(last, 0.0, pltpu.roll(x, x.shape[0] - 1, 0))


def blocks_kernel(
    n_space, feat_in, taps_in, gain_in, nbias_in, w1_in, b1_in, w2_in, b2_in, scale_in, out,
    feat, taps, gain, nbias, w1, b1, w2, b2, scale, taps32, xf, filt, mid, last_rows, halo, gathered, centers, normed, hidden,
    pair_out, pair_in, cross_out, cross_in, own,
    w_sem, in_sem, out_sem, halo_send, halo_recv, ag_send, ag_recv, pair_send, pair_recv, cross_send, cross_recv,
):
    rows, width, share = feat.shape
    half = TAPS // 2
    blocks = w1.shape[0]
    band = lax.axis_index("space")
    me = lax.axis_index("tensor")
    core = lax.rem(me, 2)
    mate = me + 1 - 2 * core
    across = lax.rem(me + 2, CORES)
    diagonal = lax.rem(mate + 2, CORES)
    has_up = band > 0
    has_down = band < n_space - 1

    def weight_copies(b):
        return (
            pltpu.make_async_copy(w1_in.at[b], w1.at[b], w_sem.at[b, 0]),
            pltpu.make_async_copy(w2_in.at[b], w2.at[b], w_sem.at[b, 1]),
        )

    pairs_in = (
        (feat_in, feat), (taps_in, taps), (gain_in, gain), (nbias_in, nbias),
        (b1_in, b1), (b2_in, b2), (scale_in, scale),
    )
    small_copies = [
        pltpu.make_async_copy(src, dst, in_sem.at[i]) for i, (src, dst) in enumerate(pairs_in)
    ]
    for copy in small_copies:
        copy.start()
    for b in range(blocks):
        for copy in weight_copies(b):
            copy.start()

    barrier = pltpu.get_barrier_semaphore()
    for who in (mate, across):
        pl.semaphore_signal(barrier, inc=1, device_id=(band, who), device_id_type=MESH)

    @pl.when(has_up)
    def _():
        pl.semaphore_signal(barrier, inc=1, device_id=(band - 1, me), device_id_type=MESH)

    @pl.when(has_down)
    def _():
        pl.semaphore_signal(barrier, inc=1, device_id=(band + 1, me), device_id_type=MESH)

    pl.semaphore_wait(barrier, 2 + jnp.minimum(band, 1) + jnp.minimum(n_space - 1 - band, 1))

    def remote(src, dst, send, recv, who):
        return pltpu.make_async_remote_copy(
            src_ref=src, dst_ref=dst, send_sem=send, recv_sem=recv, device_id=who, device_id_type=MESH
        )

    def halo_copy(b, source, side, i):
        row = i if side == 0 else rows - half + i
        target = (band - 1, me) if side == 0 else (band + 1, me)
        return remote(
            source.at[row], halo.at[b, side, i], halo_send.at[b, side, i], halo_recv.at[b, side, i], target
        )

    present = (has_up, has_down)

    def ag_copy(b, r, kind):
        slot, target = ((me, mate), (me, across), (across, mate))[kind % 3]
        ref = (gathered if kind < 3 else centers).at[b, r, slot]
        return remote(ref, ref, ag_send.at[b, r, kind], ag_recv.at[b, r, kind], (band, target))

    def pair_copy(b, r):
        return remote(
            pair_out.at[b, r], pair_in.at[b, r], pair_send.at[b, r], pair_recv.at[b, r], (band, mate)
        )

    def cross_copy(b, r):
        return remote(
            cross_out.at[b, r], cross_in.at[b, r], cross_send.at[b, r], cross_recv.at[b, r], (band, across)
        )

    column = lax.broadcasted_iota(jnp.int32, (width, 128), 0)
    lane = lax.broadcasted_iota(jnp.int32, (width, 128), 1)
    first, last, diag = column == 0, column == width - 1, column == lane

    def convolve(b, r, pairs):
        def part(h, fresh):
            ch = pl.ds(pl.multiple_of(h * 128, 128), 128)

            def along(j):
                total = None
                for row, tap in pairs:
                    term = xf[row, :, ch] * taps32[b, tap, pl.ds(j, 1), ch]
                    total = term if total is None else total + term
                return total

            right = shift_down(along(0), first)
            for j in range(1, half):
                right = shift_down(right + along(j), first)
            left = shift_up(along(TAPS - 1), last)
            for j in range(TAPS - 2, half, -1):
                left = shift_up(left + along(j), last)
            total = along(half) + right + left
            if not fresh:
                total = total + filt[r, :, ch]
            filt[r, :, ch] = total

        return part

    def early_rows(b):
        if b == 0:
            return range(rows)
        return range(rows - 1) if b % 2 == 1 else range(1, rows)

    def conv_own(b):
        def body(step, carry):
            r, h = step // (share // 128), lax.rem(step, share // 128)
            convolve(b, r, [(half + m, half + m - r) for m in early_rows(b)])(h, True)
            return carry

        lax.fori_loop(0, rows * (share // 128), body, 0)

    def conv_halo(b, r):
        pairs = [(half + m, half + m - r) for m in range(rows) if m not in early_rows(b)]
        for m in range(half):
            row = r + m + rows * ((r + m) // half)
            pairs.append((row, row - r))

        def body(h, carry):
            convolve(b, r, pairs)(h, False)
            return carry

        lax.fori_loop(0, share // 128, body, 0)

    def take_halo(b, upper, i):
        side, base, there = (1, 0, has_up) if upper else (0, half + rows, has_down)

        @pl.when(there)
        def _():
            halo_copy(b, mid, side, i).wait_recv()
            xf[base + i] = halo[b, side, i].astype(jnp.float32)

        @pl.when(jnp.logical_not(there))
        def _():
            xf[base + i] = jnp.zeros((width, share), jnp.float32)

    def send_filtered(b, r):
        value = filt[r]
        center = jnp.sum(value, axis=1, keepdims=True) / share
        gathered[b, r, me] = (value - center).astype(jnp.bfloat16)
        centers[b, r, me] = jnp.sum(jnp.where(diag, center, 0.0), axis=0, keepdims=True)
        for kind in (4, 1, 3, 0):
            ag_copy(b, r, kind).start()

    def normalize(b, r):
        own_means = [
            jnp.sum(jnp.where(diag, centers[b, r, s], 0.0), axis=1, keepdims=True) for s in range(CORES)
        ]
        mean = (own_means[0] + own_means[1] + own_means[2] + own_means[3]) / CORES
        deltas = [c - mean for c in own_means]
        squares = jnp.zeros((width, share), jnp.float32)
        for s in range(CORES):
            value = gathered[b, r, s].astype(jnp.float32) + deltas[s]
            squares = squares + value * value
        var = jnp.sum(squares, axis=1, keepdims=True) / (share * CORES)
        inverse = lax.rsqrt(var + 1e-06)
        for s in range(CORES):
            ch = pl.ds(s * share, share)
            value = gathered[b, r, s].astype(jnp.float32) + deltas[s]
            value = value * inverse * gain[pl.ds(b, 1), ch] + nbias[pl.ds(b, 1), ch]
            normed[:, ch] = value.astype(jnp.bfloat16)

    def expand(b):
        for n in range(w1.shape[2] // 256):
            ch = pl.ds(n * 256, 256)
            x = jnp.dot(normed[...], w1[b, :, ch], preferred_element_type=jnp.float32) + b1[pl.ds(b, 1), ch]
            hidden[:, ch] = (0.5 * x * (1.0 + lax.erf(x * 0.7071067811865476))).astype(jnp.bfloat16)

    def reduce_to(b, owner):
        ch = pl.ds(pl.multiple_of(owner * share, share), share)
        return jnp.dot(hidden[...], w2[b, :, ch], preferred_element_type=jnp.float32)

    def pair_sum(b, r):
        pair_copy(b, r).wait_recv()
        total = cross_out[b, r].astype(jnp.float32) + pair_in[b, r, 1].astype(jnp.float32)
        cross_out[b, r] = total.astype(jnp.bfloat16)
        cross_copy(b, r).start()

    def out_copy(r):
        return pltpu.make_async_copy(last_rows.at[r], out.at[r], out_sem.at[r])

    def finish(b, r):
        cross_copy(b, r).wait_recv()
        mixed = own[r] + pair_in[b, r, 0].astype(jnp.float32) + cross_in[b, r].astype(jnp.float32)
        before = (feat if b == 0 else mid)[r].astype(jnp.float32)
        new = (before + scale[pl.ds(b, 1), :] * (mixed + b2[pl.ds(b, 1), :])).astype(jnp.bfloat16)
        if b == blocks - 1:
            last_rows[r] = new
            out_copy(r).start()
            return
        mid[r] = new
        xf[half + r] = new.astype(jnp.float32)

    def send_halo(b, source, side, i):
        @pl.when(present[side])
        def _():
            halo_copy(b, source, side, i).start()

    for i in range(half):
        send_halo(0, feat_in, 1, i)
    for copy in small_copies:
        copy.wait()
    for b in range(blocks):
        taps32[b] = taps[:, :, b, :].astype(jnp.float32)
    for r in range(rows):
        xf[half + r] = feat[r].astype(jnp.float32)

    for b in range(blocks):
        downward = b % 2 == 0
        row_of = (lambda k: k) if downward else (lambda k: rows - 1 - k)
        if b == 0:
            conv_own(b)

            @pl.when(has_down)
            def _():
                for i in range(half):
                    halo_copy(0, feat_in, 1, i).wait_send()

            for i in range(half):
                send_halo(0, feat_in, 0, i)
        else:
            send_halo(b, mid, 1 if not downward else 0, half - 2 if not downward else 1)

        for i in range(half):
            take_halo(b, downward, i)

        def front(k, carry, b=b, row_of=row_of, downward=downward):
            r = row_of(k)

            @pl.when(k > 0)
            def _():
                take_halo(b, not downward, k - 1 if downward else rows - 1 - k)

            conv_halo(b, r)
            send_filtered(b, r)

            if b > 0:
                @pl.when(k == 0)
                def _():
                    send_halo(b, mid, 1 if not downward else 0, 0 if not downward else half - 1)

            return carry

        lax.fori_loop(0, rows, front, 0)
        for copy in weight_copies(b):
            copy.wait()

        def relay(r, b=b):
            for kind in (4, 1):
                ag_copy(b, r, kind).wait_recv()
                ag_copy(b, r, kind + 1).start()

        def arrive(r, b=b):
            for kind in (0, 3, 2, 5):
                ag_copy(b, r, kind).wait_recv()

        def send_partials(r, b=b):
            pair_out[b, r, 0] = reduce_to(b, mate).astype(jnp.bfloat16)
            pair_out[b, r, 1] = reduce_to(b, diagonal).astype(jnp.bfloat16)
            pair_copy(b, r).start()

        def keep_partials(r, b=b):
            own[r] = reduce_to(b, me)
            cross_out[b, r] = reduce_to(b, across).astype(jnp.bfloat16)

        def finish_and_send(k, b=b, row_of=row_of, downward=downward):
            r = row_of(k)
            finish(b, r)
            if b < blocks - 1:
                send_halo(b + 1, mid, 0 if downward else 1, r if downward else r - (rows - half))

        relay(row_of(0))

        def middle(k, carry, b=b, row_of=row_of):
            r = row_of(k)
            arrive(r)
            normalize(b, r)

            @pl.when(k > 0)
            def _():
                pair_sum(b, row_of(k - 1))

            expand(b)

            @pl.when(k < rows - 1)
            def _():
                relay(row_of(k + 1))

            send_partials(r)
            keep_partials(r)

            @pl.when(k > 1)
            def _():
                finish_and_send(k - 2)

            return carry

        lax.fori_loop(0, rows, middle, 0)
        pair_sum(b, row_of(rows - 1))
        finish_and_send(rows - 2)
        if b < blocks - 1:
            conv_own(b + 1)
        finish(b, row_of(rows - 1))
        if b < blocks - 1:
            send_halo(b + 1, mid, 1 if downward else 0, half - 1 if downward else 0)

    for r in range(rows):
        out_copy(r).wait()
    for b in range(blocks):
        for side in range(2):
            if b == 0 and side == 1:
                continue

            @pl.when(present[side])
            def _(b=b, side=side):
                for i in range(half):
                    halo_copy(b, feat_in if b == 0 else mid, side, i).wait_send()

        def drain(r, carry, b=b):
            for kind in range(6):
                ag_copy(b, r, kind).wait_send()
            pair_copy(b, r).wait_send()
            cross_copy(b, r).wait_send()
            return carry

        lax.fori_loop(0, rows, drain, 0)


def fused(n_space, features, depth_kernel, gain, nbias, w1, b1, w2, b2, scale):
    rows, width, share = features.shape
    blocks, depth, units = w1.shape
    half = TAPS // 2
    depth_kernel = jnp.transpose(depth_kernel, (1, 2, 0, 3))
    operands = (features, depth_kernel, gain, nbias, w1, b1, w2, b2, scale)
    hbm = pl.BlockSpec(memory_space=pl.ANY)
    bf, f32 = jnp.bfloat16, jnp.float32
    dma = pltpu.SemaphoreType.DMA
    return pl.pallas_call(
        functools.partial(blocks_kernel, n_space),
        out_shape=jax.ShapeDtypeStruct(features.shape, bf),
        in_specs=[hbm] * len(operands),
        out_specs=hbm,
        scratch_shapes=[
            *[pltpu.VMEM(a.shape, a.dtype) for a in operands],
            pltpu.VMEM((blocks, TAPS, TAPS, share), f32),
            pltpu.VMEM((rows + 2 * half, width, share), f32),
            pltpu.VMEM((rows, width, share), f32),
            pltpu.VMEM((rows, width, share), bf),
            pltpu.VMEM((rows, width, share), bf),
            pltpu.VMEM((blocks, 2, half, width, share), bf),
            pltpu.VMEM((blocks, rows, CORES, width, share), bf),
            pltpu.VMEM((blocks, rows, CORES, 1, width), f32),
            pltpu.VMEM((width, depth), bf),
            pltpu.VMEM((width, units), bf),
            pltpu.VMEM((blocks, rows, 2, width, share), bf),
            pltpu.VMEM((blocks, rows, 2, width, share), bf),
            pltpu.VMEM((blocks, rows, width, share), bf),
            pltpu.VMEM((blocks, rows, width, share), bf),
            pltpu.VMEM((rows, width, share), f32),
            dma((blocks, 2)),
            dma((7,)),
            dma((rows,)),
            dma((blocks, 2, half)),
            dma((blocks, 2, half)),
            dma((blocks, rows, 6)),
            dma((blocks, rows, 6)),
            dma((blocks, rows)),
            dma((blocks, rows)),
            dma((blocks, rows)),
            dma((blocks, rows)),
        ],
        compiler_params=pltpu.CompilerParams(
            collective_id=0, has_side_effects=True, vmem_limit_bytes=64 * 1024 * 1024
        ),
    )(*operands)


def solution(mesh):
    sizes = dict(mesh.shape)

    def body(features, *rest):
        if sizes["tensor"] == CORES and features.shape == (TAPS // 2 + 1, 128, 256):
            return fused(sizes["space"], features, *rest)
        return per_device(features, *rest)

    return jax.shard_map(
        body,
        mesh=mesh,
        in_specs=(
            P("space", None, "tensor"),
            P(None, None, None, "tensor"),
            P(),
            P(),
            P(None, None, "tensor"),
            P(None, "tensor"),
            P(None, "tensor", None),
            P(None, "tensor"),
            P(None, "tensor"),
        ),
        out_specs=P("space", None, "tensor"),
        check_vma=False,
    )
```
